512 devices in a mesh: depth: 32 (over y, x), strip: 16 (over z, core).
Axes of the slice: x: 4, y: 8, z: 8, core: 2. Of those that a mesh axis runs over, the one named last changes fastest.
Arguments:
- arrivals: float32 [32, 1, 4, 512, 128], P('depth', None, None, 'strip'), may hold values from -6 to 6
- feed: float32 [3, 1, 4, 512, 128], P(None, None, None, 'strip'), may hold values from -6 to 6
- velocity_index: int32 [64, 512, 128], P('depth', 'strip'), may hold values from 0 to 31
- offsets: int32 [16], replicated, may hold values from -8 to 8, as said below
- coef_table: float32 [35, 9, 2, 1, 32], replicated, may hold values from -1.8 to 1.8
Outputs:
- image: float32 [64, 16, 512, 128], P('depth', None, 'strip')
- outflow: float32 [32, 1, 4, 512, 128], P('depth', None, None, 'strip')
The draws below stay inside these ranges and needn't reach their ends.
Inputs may be any that keep to these rules, and one draw needn't show every extreme that they name: The 16 offsets are distinct, and both -8 and 8 occur among them.
All inputs are finite; a program needn't handle non-finite values.
Results may differ from the reference program's by a relative error of at most 0.00025.
Values sent between devices are 32-bit elements; how exact they have to be, the bound alone decides.
A program may use at most 64 MiB of HBM per device.

```python
import jax
import jax.numpy as jnp
from jax import lax

NY = 128
F = 1
LEVELS = 32
NOFF = 16
ORDER = 8
HMAX = 8
TICKS = 4
LAYERS = 2
NSEC = 32
NZ = 64
NX = 512
NB = 35


def draw_offsets(key, part):
    inner = jax.random.permutation(jax.random.fold_in(key, 11), 2 * HMAX - 1).astype(jnp.int32) - (HMAX - 1)
    ends = jnp.array([-HMAX, HMAX], jnp.int32)
    chosen = jnp.concatenate([ends, inner[:NOFF - 2]])
    shuffle = jax.random.permutation(jax.random.fold_in(key, 23), NOFF)
    return chosen[shuffle].astype(jnp.int32)


def set_ends(values, own_key, low, high):
    longest = values.shape.index(max(values.shape))
    spots = []
    for shift in (0, 1):
        where = [jax.random.randint(jax.random.fold_in(own_key, axis), (), 0, length) for axis, length in enumerate(values.shape)]
        where[longest] = (where[longest] + shift) % values.shape[longest]
        spots.append(tuple(where))
    return values.at[spots[0]].set(low).at[spots[1]].set(high)


def block_levels(key, dims, pieces, least, high):
    loudness, own = 1.0, jax.random.fold_in(key, 6)
    for position, blocks in pieces:
        draws = jnp.exp(jax.random.uniform(jax.random.fold_in(own, position), (blocks,), jnp.float32, least / len(pieces), high / len(pieces)))
        loudness = loudness * jnp.repeat(draws, dims[position] // blocks).reshape([-1 if axis == position else 1 for axis in range(len(dims))])
    return loudness


def noise(key, shape, scale, most, cuts=(), kind=jnp.bfloat16):
    loudness = block_levels(key, shape, cuts, -0.22, 0.18) if cuts else 1.0
    values = jax.random.normal(key, shape, jnp.float32) * scale * loudness
    return jnp.minimum(jnp.maximum(values, -most), most).astype(kind)


def setup_inputs(seed: int = 0) -> dict:
    keys = jax.random.split(jax.random.key(seed), 6)
    return {
        "arrivals": noise(keys[0], (NSEC, F, 4, NX, NY), 1.0, 6.0, ((0, 32), (3, 16)), jnp.float32),
        "feed": noise(keys[1], (TICKS - 1, F, 4, NX, NY), 1.0, 6.0, ((3, 16),), jnp.float32),
        "velocity_index": set_ends(jax.random.randint(keys[2], (NZ, NX, NY), 0, LEVELS), jax.random.fold_in(keys[2], 1), 0, LEVELS - 1).astype(jnp.int32),
        "offsets": draw_offsets(jax.random.fold_in(keys[5], 71), 0),
        "coef_table": noise(keys[4], (NB, ORDER + 1, 2, F, LEVELS), 0.3, 1.8, (), jnp.float32),
    }


def lateral(field):
    lead = [(0, 0)] * (field.ndim - 2)
    along_y = jnp.pad(field, lead + [(0, 0), (1, 1)])
    smooth_y = field + 0.5 * (along_y[..., 2:] + along_y[..., :-2])
    along_x = jnp.pad(smooth_y, lead + [(1, 1), (0, 0)])
    smooth_x = smooth_y + 0.5 * (along_x[..., 2:, :] + along_x[..., :-2, :])
    return 0.5 * smooth_x - field


def weighted(total, term, coef_re, coef_im):
    source_re = term[..., 0, :, :]
    source_im = term[..., 1, :, :]
    receiver_re = term[..., 2, :, :]
    receiver_im = term[..., 3, :, :]
    piece = jnp.stack([coef_re * source_re - coef_im * source_im,
                       coef_re * source_im + coef_im * source_re,
                       coef_re * receiver_re + coef_im * receiver_im,
                       coef_re * receiver_im - coef_im * receiver_re], axis=-3)
    return total + piece


def extrapolate(state, table, levels):
    def pick(order):
        chosen_part = table[:, order]
        chosen = jax.vmap(lambda rows, cells: jnp.take(rows, cells, axis=-1))(chosen_part, levels)
        return chosen[:, 0], chosen[:, 1]

    earlier = state
    first_re, first_im = pick(0)
    total = weighted(jnp.zeros_like(state), state, first_re, first_im)
    current = lateral(state)
    second_re, second_im = pick(1)
    total = weighted(total, current, second_re, second_im)
    for order in range(2, ORDER + 1):
        following = 2.0 * lateral(current) - earlier
        earlier, current = current, following
        coef_re, coef_im = pick(order)
        total = weighted(total, current, coef_re, coef_im)
    return total


def image_terms(state, offsets):
    padded = jnp.pad(state, [(0, 0)] * 3 + [(HMAX, HMAX), (0, 0)])
    width = state.shape[3]
    rows = []
    for index in range(NOFF):
        offset = offsets[index]
        source = lax.dynamic_slice_in_dim(padded, (HMAX - offset).astype(jnp.int32), width, axis=3)
        receiver = lax.dynamic_slice_in_dim(padded, (HMAX + offset).astype(jnp.int32), width, axis=3)
        rows.append(jnp.sum(source[:, :, 0] * receiver[:, :, 2] + source[:, :, 1] * receiver[:, :, 3], axis=1))
    return jnp.stack(rows, axis=1)


def reference(arrivals, feed, velocity_index, offsets, coef_table):
    state = arrivals
    sections = jnp.arange(NSEC, dtype=jnp.int32)
    levels_all = velocity_index.reshape(NSEC, LAYERS, NX, NY)
    image = jnp.zeros((NSEC, LAYERS, NOFF, NX, NY), jnp.float32)
    for tick in range(TICKS):
        table = coef_table[(tick - sections + NSEC - 1).astype(jnp.int32)]
        for row in range(LAYERS):
            state = extrapolate(state, table, levels_all[:, row])
            image = image.at[:, row].add(image_terms(state, offsets))
        if tick + 1 < TICKS:
            state = jnp.concatenate([feed[tick][None], state[:-1]], axis=0)
    return image.reshape(NSEC * LAYERS, NOFF, NX, NY), state
```

```python
import functools

import jax
import jax.numpy as jnp
from jax import lax
from jax.experimental import pallas as pl
from jax.experimental.pallas import tpu as pltpu
from jax.sharding import PartitionSpec as P

MESH = pl.DeviceIdType.MESH
ORDER = 8
W = 32
NY = 128
F32 = jnp.float32

ROWS = (128, 112, 96, 80, 64, 48)
LAST = (80, 64)

MSGS = {}
for _s in (1, -1, 2, -2):
    MSGS["a", _s] = (0, _s)
    MSGS["v0", _s] = (0, _s)
for _s in (0, 1, -1):
    MSGS["v1", _s] = (-1, _s)
    MSGS["v2", _s] = (-2, _s)
    MSGS["m", _s] = (3, _s)
for _s in (1, -1):
    MSGS["f1", _s] = (0, _s)
    MSGS["f2", _s] = (0, _s)
    MSGS["i2", 1, _s] = (2, _s)
for _l in (0, 1):
    MSGS["i1", _l, 0] = (1, 0)
    MSGS["i2", _l, 0] = (2, 0)
INDEX = {name: i for i, name in enumerate(MSGS)}
PEERS = sorted(set(MSGS.values()))


def layer(rows, load, lev, tab, top, total, out):
    nb = rows // 8
    lanes = lax.broadcasted_iota(jnp.int32, (8, NY), 1)
    first, final = lanes == 0, lanes == NY - 1
    blocks = lax.broadcasted_iota(jnp.int32, (8, NY), 0) * nb + top
    inside = [(blocks + j >= 0) & (blocks + j < total) for j in range(nb)]
    quarter = [jnp.where(inside[j], 0.25, 0.0) for j in range(nb)]
    comps = range(4)
    t = [[jnp.where(inside[j], load(c, j, nb), 0.0) for j in range(nb)] for c in comps]
    hist = [t]
    p = None
    for n in range(1, ORDER + 1):
        new_t, new_p = [], []
        for c in comps:
            u = t[c]
            up = pltpu.roll(u[nb - 1], 1, 0)
            down = pltpu.roll(u[0], 7, 0)
            s = [u[j] + u[j + 1] for j in range(nb - 1)]
            tl, ql = [], []
            for j in range(nb):
                a = s[j - 1] if j else up + u[0]
                b = s[j] if j + 1 < nb else u[nb - 1] + down
                v = a + b
                sides = jnp.where(first, 0.0, pltpu.roll(v, 1, 1)) + jnp.where(
                    final, 0.0, pltpu.roll(v, NY - 1, 1)
                )
                q = (v + v) + sides
                if n == 1:
                    r = q * (quarter[j] * 0.5)
                else:
                    r = q * quarter[j] - p[c][j]
                ql.append(r)
                tl.append(r - u[j])
            new_t.append(tl)
            new_p.append(ql)
        t, p = new_t, new_p
        hist.append(t)
    for j in range(nb):
        idx = lev(j, nb)
        acc = [None] * 4
        for n in range(ORDER + 1):
            cr = jnp.take_along_axis(tab[2 * n], idx, axis=1)
            ci = jnp.take_along_axis(tab[2 * n + 1], idx, axis=1)
            sr, si, rr, ri = [hist[n][c][j] for c in comps]
            new = [
                cr * sr - ci * si,
                cr * si + ci * sr,
                cr * rr + ci * ri,
                cr * ri - ci * rr,
            ]
            acc = [new[c] if n == 0 else acc[c] + new[c] for c in comps]
        for c in comps:
            out(c, j, nb, acc[c])


def kernel(depths, strips, arr, vel, offs, feed, table, img, outflow, A, V0, V1, V2, Y0, Y1, Y2, Y3, Y4, Y5, Y6, Y7, M, I1, I2, TB, TW, ssem, rsem, lsem, tsem):
    d = lax.axis_index("depth")
    s = lax.axis_index("strip")

    def peer(shift):
        return (
            lax.rem(d + shift[0] + depths, depths),
            lax.rem(s + shift[1] + strips, strips),
        )

    barrier = pltpu.get_barrier_semaphore()
    for shift in PEERS:
        pl.semaphore_signal(barrier, inc=1, device_id=peer((-shift[0], -shift[1])), device_id_type=MESH)

    wraps = [d + k >= depths for k in range(3)]
    tick_row = [jnp.where(wraps[k], 2 * depths - 1 - d, depths - 1 - d) for k in range(3)] + [depths + 2 - d]
    tabs = [pltpu.make_async_copy(table.at[tick_row[k]], TB.at[k], tsem.at[k]) for k in range(4)]
    for copy in tabs:
        copy.start()

    def send(name, src, dst):
        i = INDEX[name]
        return pltpu.make_async_remote_copy(
            src_ref=src, dst_ref=dst, send_sem=ssem.at[i], recv_sem=rsem.at[i],
            device_id=peer(MSGS[name]), device_id_type=MESH,
        )

    def rows(ref, start, count, lead=()):
        return ref.at[(*lead, slice(None), pl.ds(start, count), slice(None))]

    own = arr.at[0, 0]
    lead1, lead2 = A.shape[1] // 2 - W // 2, V2.shape[1] // 2 - W // 2
    sends = {}
    sends["v0", 1] = (vel, rows(V0, 16, 32))
    sends["v0", -1] = (vel, rows(V0, 80, 32))
    sends["v0", 2] = (rows(vel, 16, 16), rows(V0, 0, 16))
    sends["v0", -2] = (rows(vel, 0, 16), rows(V0, 112, 16))
    sends["a", 1] = (own, rows(A, 16, 32))
    sends["a", -1] = (own, rows(A, 80, 32))
    sends["a", 2] = (rows(arr, 16, 16, (0, 0)), rows(A, 0, 16))
    sends["a", -2] = (rows(arr, 0, 16, (0, 0)), rows(A, 112, 16))
    sends["v1", 0] = (vel, rows(V1, 32, 32))
    sends["v1", 1] = (vel, rows(V1, 0, 32))
    sends["v1", -1] = (vel, rows(V1, 64, 32))
    sends["v2", 0] = (vel, rows(V2, 16, 32))
    sends["v2", 1] = (rows(vel, 16, 16), rows(V2, 0, 16))
    sends["v2", -1] = (rows(vel, 0, 16), rows(V2, 48, 16))
    for layer_ in (0, 1):
        sends["i1", layer_, 0] = (rows((Y2, Y3)[layer_], (24, 16)[layer_], 48, () if layer_ == 0 else (0,)), I1.at[layer_])
    sends["i2", 0, 0] = (rows(Y4, 8, 48), I2.at[0])
    sends["i2", 1, 0] = (rows(Y5, 8, 32), rows(I2, 8, 32, (1,)))
    sends["i2", 1, 1] = (rows(Y5, 32, 8), rows(I2, 0, 8, (1,)))
    sends["i2", 1, -1] = (rows(Y5, 8, 8), rows(I2, 40, 8, (1,)))
    moved = {0: (8, 32, 24), 1: (16, 24, 0), -1: (8, 24, 56)}
    for shift, (start, count, to) in moved.items():
        sends["m", shift] = (rows(Y5, start, count), rows(M, to, count))
    for shift, to in ((1, 8), (-1, 72)):
        sends["f1", shift] = (feed.at[0, 0], rows(Y1, to, 32, (1,)))
    sends["f2", 1] = (rows(feed, 16, 16, (1, 0)), rows(Y3, 8, 16, (1,)))
    sends["f2", -1] = (rows(feed, 0, 16, (1, 0)), rows(Y3, 56, 16, (1,)))
    copies = {name: send(name, *ends) for name, ends in sends.items()}

    def start(kind):
        for name in copies:
            if name[0] == kind:
                copies[name].start()

    def received(*kind):
        for name in copies:
            if name[: len(kind)] == kind:
                copies[name].wait_recv()

    fed1 = pltpu.make_async_copy(feed.at[0, 0], rows(Y1, 40, 32, (1,)), lsem.at[0])
    fed2 = pltpu.make_async_copy(feed.at[1, 0], rows(Y3, 24, 32, (1,)), lsem.at[1])
    fed3 = pltpu.make_async_copy(feed.at[2, 0], rows(Y5, 8, 32), lsem.at[2])

    pl.semaphore_wait(barrier, len(PEERS))
    start("v0")
    start("a")
    start("v1")
    start("v2")

    @pl.when(d == depths - 1)
    def _():
        start("f1")
        fed1.start()

    @pl.when(d == depths - 2)
    def _():
        start("f2")
        fed2.start()

    A[:, 48:80, :] = arr[0, 0]
    V0[:, 48:80, :] = vel[...]
    for copy in tabs:
        copy.wait()
    for k in range(4):
        for n in range(ORDER + 1):
            for part in (0, 1):
                line = TB[k, n, part]
                line = jnp.concatenate([line, line, line, line], axis=1)
                TW[k, 2 * n + part] = jnp.broadcast_to(line, (8, NY))

    total = strips * W
    middle = s * W + W // 2

    def step(count, src, lead, off, lev, row, base, tick, dst, dst_lead):
        tab = [TW[tick, i] for i in range(2 * ORDER + 2)]

        def load(c, j, nb):
            return src[(*lead, c, pl.ds(off + j, 8, stride=nb), slice(None))]

        def levels(j, nb):
            return lev[row, pl.ds(base + j, 8, stride=nb), :]

        def out(c, j, nb, value):
            dst[(*dst_lead, c, pl.ds(j, 8, stride=nb), slice(None))] = value

        layer(count, load, levels, tab, middle - count // 2, total, out)

    received("v0")
    received("a")
    step(ROWS[0], A, (), 0, V0, 0, 0, 0, Y0, ())
    step(ROWS[1], Y0, (), 8, V0, 1, 8, 0, Y1, (0,))
    received("v1")

    @pl.when(d == depths - 1)
    def _():
        received("f1")
        fed1.wait()

    last1 = jnp.where(d == depths - 1, 1, 0)
    step(ROWS[2], Y1, (last1,), 8, V1, 0, 0, 1, Y2, ())
    copies["i1", 0, 0].start()
    step(ROWS[3], Y2, (), 8, V1, 1, 8, 1, Y3, (0,))
    copies["i1", 1, 0].start()
    received("v2")

    @pl.when(d == depths - 2)
    def _():
        received("f2")
        fed2.wait()

    last2 = jnp.where(d == depths - 2, 1, 0)
    step(ROWS[4], Y3, (last2,), 8, V2, 0, 0, 2, Y4, ())
    copies["i2", 0, 0].start()
    step(ROWS[5], Y4, (), 8, V2, 1, 8, 2, Y5, ())

    @pl.when(d != depths - 3)
    def _():
        start("m")

    for name in ((0, 1, 0), (0, 1, 1), (0, 1, -1)):
        copies[("i2",) + name[1:]].start()

    @pl.when(d == depths - 3)
    def _():
        for name in ((1, 0), (1, 1), (1, -1)):
            copies[("i2",) + name].wait_send()
        fed3.start()
        fed3.wait()
        start("m")

    def image(sources, fresh):
        def body(k, carry):
            h = offs[k]
            for row in (0, 1):
                value = None if fresh else img[row, k]
                for ref, lead, at in sources[row]:
                    low = [ref[(*lead, c, pl.ds(at - h, W), slice(None))] for c in (0, 1)]
                    high = [ref[(*lead, c, pl.ds(at + h, W), slice(None))] for c in (2, 3)]
                    piece = low[0] * high[0] + low[1] * high[1]
                    value = piece if value is None else value + piece
                img[row, k] = value
            return carry

        lax.fori_loop(0, img.shape[1], body, 0)

    image([[(Y0, (), 48)], [(Y1, (0,), 40)]], True)
    received("i1")
    image([[(I1, (0,), 8)], [(I1, (1,), 8)]], False)
    received("i2")

    @pl.when(s == 0)
    def _():
        I2[1, :, 0:8, :] = jnp.zeros((4, 8, NY), F32)

    @pl.when(s == strips - 1)
    def _():
        I2[1, :, 40:48, :] = jnp.zeros((4, 8, NY), F32)

    image([[(I2, (0,), 8)], [(I2, (1,), 8)]], False)

    received("m")
    step(LAST[0], M, (), 0, V0, 0, 24, 3, Y6, ())
    step(LAST[1], Y6, (), 8, V0, 1, 32, 3, Y7, ())
    outflow[0, 0] = Y7[:, 16:48, :]
    image([[(Y6, (), 24)], [(Y7, (), 16)]], False)

    for name in copies:
        if name[0] in ("a", "v0", "v1", "v2", "i1", "m") or name == ("i2", 0, 0):
            copies[name].wait_send()

    @pl.when(d == depths - 1)
    def _():
        for shift in (1, -1):
            copies["f1", shift].wait_send()

    @pl.when(d == depths - 2)
    def _():
        for shift in (1, -1):
            copies["f2", shift].wait_send()

    @pl.when(d != depths - 3)
    def _():
        for name in ((1, 0), (1, 1), (1, -1)):
            copies[("i2",) + name].wait_send()


def solution(mesh):
    depths, strips = mesh.shape["depth"], mesh.shape["strip"]

    def per_device(arrivals, feed, velocity_index, offsets, coef_table):
        vmem = pl.BlockSpec(memory_space=pltpu.VMEM)
        field = lambda n, *lead: pltpu.VMEM((*lead, 4, n, NY), F32)
        level = lambda n: pltpu.VMEM((2, n, NY), jnp.int32)
        noff = offsets.shape[0]
        return pl.pallas_call(
            functools.partial(kernel, depths, strips),
            out_shape=(
                jax.ShapeDtypeStruct((2, noff, W, NY), F32),
                jax.ShapeDtypeStruct((1, 1, 4, W, NY), F32),
            ),
            in_specs=[vmem, vmem, pl.BlockSpec(memory_space=pltpu.SMEM), pl.BlockSpec(memory_space=pl.ANY), pl.BlockSpec(memory_space=pl.ANY)],
            out_specs=(vmem, vmem),
            scratch_shapes=[
                field(128), level(128), level(96), level(64),
                field(128), field(112, 2), field(96), field(80, 2), field(64), field(48), field(80), field(64),
                field(80), field(48, 2), field(48, 2),
                pltpu.VMEM((4, ORDER + 1, 2, 1, 32), F32),
                pltpu.VMEM((4, 2 * ORDER + 2, 8, NY), F32),
                pltpu.SemaphoreType.DMA((len(MSGS),)),
                pltpu.SemaphoreType.DMA((len(MSGS),)),
                pltpu.SemaphoreType.DMA((3,)),
                pltpu.SemaphoreType.DMA((4,)),
            ],
            compiler_params=pltpu.CompilerParams(collective_id=0, has_side_effects=True, vmem_limit_bytes=48 * 2**20),
            name="relay",
        )(arrivals, velocity_index, offsets, feed, coef_table)

    return jax.shard_map(
        per_device,
        mesh=mesh,
        in_specs=(
            P("depth", None, None, "strip", None),
            P(None, None, None, "strip", None),
            P("depth", "strip", None),
            P(),
            P(),
        ),
        out_specs=(P("depth", None, "strip", None), P("depth", None, None, "strip", None)),
        check_vma=False,
    )
```

```python
import functools

import jax
import jax.numpy as jnp
from jax import lax
from jax.experimental import pallas as pl
from jax.experimental.pallas import tpu as pltpu
from jax.sharding import PartitionSpec as P

MESH = pl.DeviceIdType.MESH
ORDER = 8
W = 32
NY = 128
LEVELS = 32
TABS = (2 * (ORDER + 1) * LEVELS + NY - 1) // NY
F32 = jnp.float32

ROWS = (128, 112, 96, 80, 64, 48)
LAST = (80, 64)

MSGS = {}
for _s in (1, -1, 2, -2):
    MSGS["a", _s] = (0, _s)
    MSGS["v0", _s] = (0, _s)
for _s in (0, 1, -1):
    MSGS["v1", _s] = (-1, _s)
    MSGS["v2", _s] = (-2, _s)
    MSGS["m", _s] = (3, _s)
for _s in (1, -1):
    MSGS["f1", _s] = (0, _s)
    MSGS["f2", _s] = (0, _s)
    MSGS["i2", 1, _s] = (2, _s)
for _l in (0, 1):
    MSGS["i1", _l, 0] = (1, 0)
    MSGS["i2", _l, 0] = (2, 0)
INDEX = {name: i for i, name in enumerate(MSGS)}
PEERS = sorted(set(MSGS.values()))


def layer(rows, load, lev, tab, top, total, out):
    nb = rows // 8
    lanes = lax.broadcasted_iota(jnp.int32, (8, NY), 1)
    first, final = lanes == 0, lanes == NY - 1
    blocks = lax.broadcasted_iota(jnp.int32, (8, NY), 0) * nb + top
    inside = [(blocks + j >= 0) & (blocks + j < total) for j in range(nb)]
    quarter = [jnp.where(inside[j], 0.25, 0.0) for j in range(nb)]
    comps = range(4)
    t = [[jnp.where(inside[j], load(c, j, nb), 0.0) for j in range(nb)] for c in comps]
    hist = [t]
    p = None
    for n in range(1, ORDER + 1):
        new_t, new_p = [], []
        for c in comps:
            u = t[c]
            up = pltpu.roll(u[nb - 1], 1, 0)
            down = pltpu.roll(u[0], 7, 0)
            s = [u[j] + u[j + 1] for j in range(nb - 1)]
            tl, ql = [], []
            for j in range(nb):
                a = s[j - 1] if j else up + u[0]
                b = s[j] if j + 1 < nb else u[nb - 1] + down
                v = a + b
                sides = jnp.where(first, 0.0, pltpu.roll(v, 1, 1)) + jnp.where(
                    final, 0.0, pltpu.roll(v, NY - 1, 1)
                )
                q = (v + v) + sides
                if n == 1:
                    r = q * (quarter[j] * 0.5)
                else:
                    r = q * quarter[j] - p[c][j]
                ql.append(r)
                tl.append(r - u[j])
            new_t.append(tl)
            new_p.append(ql)
        t, p = new_t, new_p
        hist.append(t)
    for j in range(nb):
        idx = lev(j, nb)
        idx = [idx + LEVELS * m for m in range(4)]
        acc = [None] * 4
        for n in range(ORDER + 1):
            cr, ci = [
                jnp.take_along_axis(tab[c // 4], idx[c % 4], axis=1) for c in (2 * n, 2 * n + 1)
            ]
            sr, si, rr, ri = [hist[n][c][j] for c in comps]
            new = [
                cr * sr - ci * si,
                cr * si + ci * sr,
                cr * rr + ci * ri,
                cr * ri - ci * rr,
            ]
            acc = [new[c] if n == 0 else acc[c] + new[c] for c in comps]
        for c in comps:
            out(c, j, nb, acc[c])


def kernel(depths, strips, arr, vel, offs, feed, table, img, outflow, A, V0, V1, V2, Y0, Y1, Y2, Y3, Y4, Y5, Y6, Y7, M, I1, I2, TC, TT, TW, ssem, rsem, lsem):
    d = lax.axis_index("depth")
    s = lax.axis_index("strip")

    def peer(shift):
        return (
            lax.rem(d + shift[0] + depths, depths),
            s + shift[1],
        )

    def there(shift, sign=1):
        if shift[1] == 0:
            return None
        at = s + sign * shift[1]
        return (at >= 0) & (at < strips)

    def guarded(condition, action):
        if condition is None:
            action()
        else:
            pl.when(condition)(action)

    loads = [
        pltpu.make_async_copy(table, TC, lsem.at[3]),
        pltpu.make_async_copy(arr.at[0, 0], A.at[:, pl.ds(48, 32), :], lsem.at[4]),
        pltpu.make_async_copy(vel, V0.at[:, pl.ds(48, 32), :], lsem.at[5]),
    ]
    for copy in loads:
        copy.start()

    @pl.when(s < 2)
    def _():
        V0[:, 0:48, :] = jnp.zeros((2, 48, NY), jnp.int32)
        V1[:, 0:32, :] = jnp.zeros((2, 32, NY), jnp.int32)
        V2[:, 0:16, :] = jnp.zeros((2, 16, NY), jnp.int32)

    @pl.when(s >= strips - 2)
    def _():
        V0[:, 80:128, :] = jnp.zeros((2, 48, NY), jnp.int32)
        V1[:, 64:96, :] = jnp.zeros((2, 32, NY), jnp.int32)
        V2[:, 48:64, :] = jnp.zeros((2, 16, NY), jnp.int32)

    barrier = pltpu.get_barrier_semaphore()
    expected = 0
    for shift in PEERS:
        def greet(shift=shift):
            pl.semaphore_signal(barrier, inc=1, device_id=peer((-shift[0], -shift[1])), device_id_type=MESH)

        guarded(there(shift, -1), greet)
        expected = expected + (1 if shift[1] == 0 else jnp.where(there(shift), 1, 0))

    def send(name, src, dst):
        i = INDEX[name]
        return pltpu.make_async_remote_copy(
            src_ref=src, dst_ref=dst, send_sem=ssem.at[i], recv_sem=rsem.at[i],
            device_id=peer(MSGS[name]), device_id_type=MESH,
        )

    def rows(ref, start, count, lead=()):
        return ref.at[(*lead, slice(None), pl.ds(start, count), slice(None))]

    own = arr.at[0, 0]
    lead1, lead2 = A.shape[1] // 2 - W // 2, V2.shape[1] // 2 - W // 2
    sends = {}
    sends["v0", 1] = (vel, rows(V0, 16, 32))
    sends["v0", -1] = (vel, rows(V0, 80, 32))
    sends["v0", 2] = (rows(vel, 16, 16), rows(V0, 0, 16))
    sends["v0", -2] = (rows(vel, 0, 16), rows(V0, 112, 16))
    sends["a", 1] = (own, rows(A, 16, 32))
    sends["a", -1] = (own, rows(A, 80, 32))
    sends["a", 2] = (rows(arr, 16, 16, (0, 0)), rows(A, 0, 16))
    sends["a", -2] = (rows(arr, 0, 16, (0, 0)), rows(A, 112, 16))
    sends["v1", 0] = (vel, rows(V1, 32, 32))
    sends["v1", 1] = (vel, rows(V1, 0, 32))
    sends["v1", -1] = (vel, rows(V1, 64, 32))
    sends["v2", 0] = (vel, rows(V2, 16, 32))
    sends["v2", 1] = (rows(vel, 16, 16), rows(V2, 0, 16))
    sends["v2", -1] = (rows(vel, 0, 16), rows(V2, 48, 16))
    for layer_ in (0, 1):
        sends["i1", layer_, 0] = (rows((Y2, Y3)[layer_], (24, 16)[layer_], 48, () if layer_ == 0 else (0,)), I1.at[layer_])
    sends["i2", 0, 0] = (rows(Y4, 8, 48), I2.at[0])
    sends["i2", 1, 0] = (rows(Y5, 8, 32), rows(I2, 8, 32, (1,)))
    sends["i2", 1, 1] = (rows(Y5, 32, 8), rows(I2, 0, 8, (1,)))
    sends["i2", 1, -1] = (rows(Y5, 8, 8), rows(I2, 40, 8, (1,)))
    moved = {0: (8, 32, 24), 1: (16, 24, 0), -1: (8, 24, 56)}
    for shift, (start, count, to) in moved.items():
        sends["m", shift] = (rows(Y5, start, count), rows(M, to, count))
    for shift, to in ((1, 8), (-1, 72)):
        sends["f1", shift] = (feed.at[0, 0], rows(Y1, to, 32, (1,)))
    sends["f2", 1] = (rows(feed, 16, 16, (1, 0)), rows(Y3, 8, 16, (1,)))
    sends["f2", -1] = (rows(feed, 0, 16, (1, 0)), rows(Y3, 56, 16, (1,)))
    copies = {name: send(name, *ends) for name, ends in sends.items()}

    def start(kind):
        for name in copies:
            if name[0] == kind:
                guarded(there(MSGS[name]), copies[name].start)

    def received(*kind):
        for name in copies:
            if name[: len(kind)] == kind:
                guarded(there(MSGS[name], -1), copies[name].wait_recv)

    def sent(name):
        guarded(there(MSGS[name]), copies[name].wait_send)

    fed1 = pltpu.make_async_copy(feed.at[0, 0], rows(Y1, 40, 32, (1,)), lsem.at[0])
    fed2 = pltpu.make_async_copy(feed.at[1, 0], rows(Y3, 24, 32, (1,)), lsem.at[1])
    fed3 = pltpu.make_async_copy(feed.at[2, 0], rows(Y5, 8, 32), lsem.at[2])

    pl.semaphore_wait(barrier, expected)
    start("v0")
    start("a")
    start("v1")
    start("v2")

    @pl.when(d == depths - 1)
    def _():
        start("f1")
        fed1.start()

    @pl.when(d == depths - 2)
    def _():
        start("f2")
        fed2.start()

    for copy in loads:
        copy.wait()
    turned = TC[...].T
    for g in range(TABS):
        width = min(NY, table.shape[0] - g * NY)
        TT[g, :, 0:width] = turned[:, g * NY : g * NY + width]
    wraps = [d + k >= depths for k in range(3)]
    tick_row = [jnp.where(wraps[k], 2 * depths - 1 - d, depths - 1 - d) for k in range(3)] + [depths + 2 - d]
    for k in range(4):
        for g in range(TABS):
            line = TT[g, pl.ds(tick_row[k], 1), :]
            TW[k, g] = jnp.broadcast_to(line, (8, NY))

    total = strips * W
    middle = s * W + W // 2

    def step(count, src, lead, off, lev, row, base, tick, dst, dst_lead):
        tab = [TW[tick, g] for g in range(TABS)]

        def load(c, j, nb):
            return src[(*lead, c, pl.ds(off + j, 8, stride=nb), slice(None))]

        def levels(j, nb):
            return lev[row, pl.ds(base + j, 8, stride=nb), :]

        def out(c, j, nb, value):
            dst[(*dst_lead, c, pl.ds(j, 8, stride=nb), slice(None))] = value

        layer(count, load, levels, tab, middle - count // 2, total, out)

    received("v0")
    received("a")
    step(ROWS[0], A, (), 0, V0, 0, 0, 0, Y0, ())
    step(ROWS[1], Y0, (), 8, V0, 1, 8, 0, Y1, (0,))
    received("v1")

    @pl.when(d == depths - 1)
    def _():
        received("f1")
        fed1.wait()

    last1 = jnp.where(d == depths - 1, 1, 0)
    step(ROWS[2], Y1, (last1,), 8, V1, 0, 0, 1, Y2, ())
    copies["i1", 0, 0].start()
    step(ROWS[3], Y2, (), 8, V1, 1, 8, 1, Y3, (0,))
    copies["i1", 1, 0].start()
    received("v2")

    @pl.when(d == depths - 2)
    def _():
        received("f2")
        fed2.wait()

    last2 = jnp.where(d == depths - 2, 1, 0)
    step(ROWS[4], Y3, (last2,), 8, V2, 0, 0, 2, Y4, ())
    copies["i2", 0, 0].start()
    step(ROWS[5], Y4, (), 8, V2, 1, 8, 2, Y5, ())

    @pl.when(d != depths - 3)
    def _():
        start("m")

    for name in ((0, 1, 0), (0, 1, 1), (0, 1, -1)):
        guarded(there(MSGS[("i2",) + name[1:]]), copies[("i2",) + name[1:]].start)

    @pl.when(d == depths - 3)
    def _():
        for name in ((1, 0), (1, 1), (1, -1)):
            sent(("i2",) + name)
        fed3.start()
        fed3.wait()
        start("m")

    def image(sources, fresh):
        def body(k, carry):
            h = offs[k]
            for row in (0, 1):
                value = None if fresh else img[row, k]
                for ref, lead, at in sources[row]:
                    low = [ref[(*lead, c, pl.ds(at - h, W), slice(None))] for c in (0, 1)]
                    high = [ref[(*lead, c, pl.ds(at + h, W), slice(None))] for c in (2, 3)]
                    piece = low[0] * high[0] + low[1] * high[1]
                    value = piece if value is None else value + piece
                img[row, k] = value
            return carry

        lax.fori_loop(0, img.shape[1], body, 0)

    image([[(Y0, (), 48)], [(Y1, (0,), 40)]], True)
    received("i1")
    image([[(I1, (0,), 8)], [(I1, (1,), 8)]], False)
    received("i2")

    @pl.when(s == 0)
    def _():
        I2[1, :, 0:8, :] = jnp.zeros((4, 8, NY), F32)

    @pl.when(s == strips - 1)
    def _():
        I2[1, :, 40:48, :] = jnp.zeros((4, 8, NY), F32)

    image([[(I2, (0,), 8)], [(I2, (1,), 8)]], False)

    received("m")
    step(LAST[0], M, (), 0, V0, 0, 24, 3, Y6, ())
    step(LAST[1], Y6, (), 8, V0, 1, 32, 3, Y7, ())
    outflow[0, 0] = Y7[:, 16:48, :]
    image([[(Y6, (), 24)], [(Y7, (), 16)]], False)

    for name in copies:
        if name[0] in ("a", "v0", "v1", "v2", "i1", "m") or name == ("i2", 0, 0):
            sent(name)

    @pl.when(d == depths - 1)
    def _():
        for shift in (1, -1):
            sent(("f1", shift))

    @pl.when(d == depths - 2)
    def _():
        for shift in (1, -1):
            sent(("f2", shift))

    @pl.when(d != depths - 3)
    def _():
        for name in ((1, 0), (1, 1), (1, -1)):
            sent(("i2",) + name)


def solution(mesh):
    depths, strips = mesh.shape["depth"], mesh.shape["strip"]

    def per_device(arrivals, feed, velocity_index, offsets, coef_table):
        vmem = pl.BlockSpec(memory_space=pltpu.VMEM)
        anyw = pl.BlockSpec(memory_space=pl.ANY)
        field = lambda n, *lead: pltpu.VMEM((*lead, 4, n, NY), F32)
        level = lambda n: pltpu.VMEM((2, n, NY), jnp.int32)
        noff = offsets.shape[0]
        columns = jnp.transpose(coef_table, (1, 2, 3, 4, 0)).reshape(-1, coef_table.shape[0])
        return pl.pallas_call(
            functools.partial(kernel, depths, strips),
            out_shape=(
                jax.ShapeDtypeStruct((2, noff, W, NY), F32),
                jax.ShapeDtypeStruct((1, 1, 4, W, NY), F32),
            ),
            in_specs=[anyw, anyw, pl.BlockSpec(memory_space=pltpu.SMEM), anyw, anyw],
            out_specs=(vmem, vmem),
            scratch_shapes=[
                field(128), level(128), level(96), level(64),
                field(128), field(112, 2), field(96), field(80, 2), field(64), field(48), field(80), field(64),
                field(80), field(48, 2), field(48, 2),
                pltpu.VMEM(columns.shape, F32),
                pltpu.VMEM((TABS, coef_table.shape[0], NY), F32),
                pltpu.VMEM((4, TABS, 8, NY), F32),
                pltpu.SemaphoreType.DMA((len(MSGS),)),
                pltpu.SemaphoreType.DMA((len(MSGS),)),
                pltpu.SemaphoreType.DMA((6,)),
            ],
            compiler_params=pltpu.CompilerParams(collective_id=0, has_side_effects=True, vmem_limit_bytes=60 * 2**20),
            name="relay",
        )(arrivals, velocity_index, offsets, feed, columns)

    return jax.shard_map(
        per_device,
        mesh=mesh,
        in_specs=(
            P("depth", None, None, "strip", None),
            P(None, None, None, "strip", None),
            P("depth", "strip", None),
            P(),
            P(),
        ),
        out_specs=(P("depth", None, "strip", None), P("depth", None, None, "strip", None)),
        check_vma=False,
    )
```

```python
import functools

import jax
import jax.numpy as jnp
from jax import lax
from jax.experimental import pallas as pl
from jax.experimental.pallas import tpu as pltpu
from jax.sharding import PartitionSpec as P

MESH = pl.DeviceIdType.MESH
ORDER = 8
W = 32
NY = 128
LEVELS = 32
TABS = (2 * (ORDER + 1) * LEVELS + NY - 1) // NY
F32 = jnp.float32

ROWS = (128, 112, 96, 80, 64, 48)
LAST = (80, 64)

MSGS = {}
for _s in (1, -1, 2, -2):
    MSGS["a", _s] = (0, _s)
    MSGS["v0", _s] = (0, _s)
for _s in (0, 1, -1):
    MSGS["v1", _s] = (-1, _s)
    MSGS["v2", _s] = (-2, _s)
    MSGS["m", _s] = (3, _s)
for _s in (1, -1):
    MSGS["f1", _s] = (0, _s)
    MSGS["f2", _s] = (0, _s)
    MSGS["i2", 1, _s] = (2, _s)
for _l in (0, 1):
    MSGS["i1", _l, 0] = (1, 0)
    MSGS["i2", _l, 0] = (2, 0)
INDEX = {name: i for i, name in enumerate(MSGS)}
PEERS = sorted(set(MSGS.values()))


def looked_up(nb, lev, tab, j):
    idx = lev(j, nb)
    idx = [idx + LEVELS * m for m in range(4)]
    return [jnp.take_along_axis(tab[c // 4], idx[c % 4], axis=1) for c in range(2 * ORDER + 2)]


def layer(rows, load, coefs, top, total, out):
    nb = rows // 8
    lanes = lax.broadcasted_iota(jnp.int32, (8, NY), 1)
    first, final = lanes == 0, lanes == NY - 1
    blocks = lax.broadcasted_iota(jnp.int32, (8, NY), 0) * nb + top
    inside = [(blocks + j >= 0) & (blocks + j < total) for j in range(nb)]
    quarter = [jnp.where(inside[j], 0.25, 0.0) for j in range(nb)]
    comps = range(4)
    t = [[jnp.where(inside[j], load(c, j, nb), 0.0) for j in range(nb)] for c in comps]
    hist = [t]
    p = None
    for n in range(1, ORDER + 1):
        new_t, new_p = [], []
        for c in comps:
            u = t[c]
            up = pltpu.roll(u[nb - 1], 1, 0)
            down = pltpu.roll(u[0], 7, 0)
            s = [u[j] + u[j + 1] for j in range(nb - 1)]
            tl, ql = [], []
            for j in range(nb):
                a = s[j - 1] if j else up + u[0]
                b = s[j] if j + 1 < nb else u[nb - 1] + down
                v = a + b
                sides = jnp.where(first, 0.0, pltpu.roll(v, 1, 1)) + jnp.where(
                    final, 0.0, pltpu.roll(v, NY - 1, 1)
                )
                q = (v + v) + sides
                if n == 1:
                    r = q * (quarter[j] * 0.5)
                else:
                    r = q * quarter[j] - p[c][j]
                ql.append(r)
                tl.append(r - u[j])
            new_t.append(tl)
            new_p.append(ql)
        t, p = new_t, new_p
        hist.append(t)
    for j in range(nb):
        chosen = coefs(j)
        acc = [None] * 4
        for n in range(ORDER + 1):
            cr, ci = chosen[2 * n], chosen[2 * n + 1]
            sr, si, rr, ri = [hist[n][c][j] for c in comps]
            new = [
                cr * sr - ci * si,
                cr * si + ci * sr,
                cr * rr + ci * ri,
                cr * ri - ci * rr,
            ]
            acc = [new[c] if n == 0 else acc[c] + new[c] for c in comps]
        for c in comps:
            out(c, j, nb, acc[c])


def product(ref, lead, at, h):
    low = [ref[(*lead, c, pl.ds(at - h, W), slice(None))] for c in (0, 1)]
    high = [ref[(*lead, c, pl.ds(at + h, W), slice(None))] for c in (2, 3)]
    return low[0] * high[0] + low[1] * high[1]


def finish(partial, last, offs, image, outflow, out, fields, sem):
    loads = [
        pltpu.make_async_copy(last.at[0], fields.at[0], sem.at[0]),
        pltpu.make_async_copy(last.at[1], fields.at[1], sem.at[1]),
        pltpu.make_async_copy(partial.at[0], out.at[0], sem.at[2]),
        pltpu.make_async_copy(partial.at[1], out.at[1], sem.at[3]),
    ]
    for copy in loads:
        copy.start()
    loads[1].wait()
    stores = [pltpu.make_async_copy(fields.at[1, :, pl.ds(8, W), :], outflow.at[0, 0], sem.at[6])]
    stores[0].start()
    loads[0].wait()
    for row in (0, 1):
        loads[2 + row].wait()

        def body(k, carry):
            out[row, k] = out[row, k] + product(fields, (row,), 8, offs[k])
            return carry

        lax.fori_loop(0, out.shape[1], body, 0)
        stores.append(pltpu.make_async_copy(out.at[row], image.at[row], sem.at[4 + row]))
        stores[-1].start()
    for copy in stores:
        copy.wait()


def kernel(depths, strips, arr, vel, offs, feed, table, img_out, last_out, img, A, V0, V1, V2, Y0, Y1, Y2, Y3, Y4, Y5, Y6, Y7, M, I1, I2, TC, TT, TW, C6, C7, ssem, rsem, lsem):
    d = lax.axis_index("depth")
    s = lax.axis_index("strip")

    def peer(shift):
        return (
            lax.rem(d + shift[0] + depths, depths),
            s + shift[1],
        )

    def there(shift, sign=1):
        if shift[1] == 0:
            return None
        at = s + sign * shift[1]
        return (at >= 0) & (at < strips)

    def guarded(condition, action):
        if condition is None:
            action()
        else:
            pl.when(condition)(action)

    loads = [
        pltpu.make_async_copy(table, TC, lsem.at[3]),
        pltpu.make_async_copy(arr.at[0, 0], A.at[:, pl.ds(48, 32), :], lsem.at[4]),
        pltpu.make_async_copy(vel, V0.at[:, pl.ds(48, 32), :], lsem.at[5]),
    ]
    for copy in loads:
        copy.start()

    @pl.when(s < 2)
    def _():
        V0[:, 0:48, :] = jnp.zeros((2, 48, NY), jnp.int32)
        V1[:, 0:32, :] = jnp.zeros((2, 32, NY), jnp.int32)
        V2[:, 0:16, :] = jnp.zeros((2, 16, NY), jnp.int32)

    @pl.when(s >= strips - 2)
    def _():
        V0[:, 80:128, :] = jnp.zeros((2, 48, NY), jnp.int32)
        V1[:, 64:96, :] = jnp.zeros((2, 32, NY), jnp.int32)
        V2[:, 48:64, :] = jnp.zeros((2, 16, NY), jnp.int32)

    barrier = pltpu.get_barrier_semaphore()
    expected = 0
    for shift in PEERS:
        def greet(shift=shift):
            pl.semaphore_signal(barrier, inc=1, device_id=peer((-shift[0], -shift[1])), device_id_type=MESH)

        guarded(there(shift, -1), greet)
        expected = expected + (1 if shift[1] == 0 else jnp.where(there(shift), 1, 0))

    def send(name, src, dst):
        i = INDEX[name]
        return pltpu.make_async_remote_copy(
            src_ref=src, dst_ref=dst, send_sem=ssem.at[i], recv_sem=rsem.at[i],
            device_id=peer(MSGS[name]), device_id_type=MESH,
        )

    def rows(ref, start, count, lead=()):
        return ref.at[(*lead, slice(None), pl.ds(start, count), slice(None))]

    own = arr.at[0, 0]
    lead1, lead2 = A.shape[1] // 2 - W // 2, V2.shape[1] // 2 - W // 2
    sends = {}
    sends["v0", 1] = (vel, rows(V0, 16, 32))
    sends["v0", -1] = (vel, rows(V0, 80, 32))
    sends["v0", 2] = (rows(vel, 16, 16), rows(V0, 0, 16))
    sends["v0", -2] = (rows(vel, 0, 16), rows(V0, 112, 16))
    sends["a", 1] = (own, rows(A, 16, 32))
    sends["a", -1] = (own, rows(A, 80, 32))
    sends["a", 2] = (rows(arr, 16, 16, (0, 0)), rows(A, 0, 16))
    sends["a", -2] = (rows(arr, 0, 16, (0, 0)), rows(A, 112, 16))
    sends["v1", 0] = (vel, rows(V1, 32, 32))
    sends["v1", 1] = (vel, rows(V1, 0, 32))
    sends["v1", -1] = (vel, rows(V1, 64, 32))
    sends["v2", 0] = (vel, rows(V2, 16, 32))
    sends["v2", 1] = (rows(vel, 16, 16), rows(V2, 0, 16))
    sends["v2", -1] = (rows(vel, 0, 16), rows(V2, 48, 16))
    for layer_ in (0, 1):
        sends["i1", layer_, 0] = (rows((Y2, Y3)[layer_], (24, 16)[layer_], 48, () if layer_ == 0 else (0,)), I1.at[layer_])
    sends["i2", 0, 0] = (rows(Y4, 8, 48), I2.at[0])
    sends["i2", 1, 0] = (rows(Y5, 8, 32), rows(I2, 8, 32, (1,)))
    sends["i2", 1, 1] = (rows(Y5, 32, 8), rows(I2, 0, 8, (1,)))
    sends["i2", 1, -1] = (rows(Y5, 8, 8), rows(I2, 40, 8, (1,)))
    moved = {0: (8, 32, 24), 1: (16, 24, 0), -1: (8, 24, 56)}
    for shift, (start, count, to) in moved.items():
        sends["m", shift] = (rows(Y5, start, count), rows(M, to, count))
    for shift, to in ((1, 8), (-1, 72)):
        sends["f1", shift] = (feed.at[0, 0], rows(Y1, to, 32, (1,)))
    sends["f2", 1] = (rows(feed, 16, 16, (1, 0)), rows(Y3, 8, 16, (1,)))
    sends["f2", -1] = (rows(feed, 0, 16, (1, 0)), rows(Y3, 56, 16, (1,)))
    copies = {name: send(name, *ends) for name, ends in sends.items()}

    def start(kind):
        for name in copies:
            if name[0] == kind:
                guarded(there(MSGS[name]), copies[name].start)

    def received(*kind):
        for name in copies:
            if name[: len(kind)] == kind:
                guarded(there(MSGS[name], -1), copies[name].wait_recv)

    def sent(name):
        guarded(there(MSGS[name]), copies[name].wait_send)

    fed1 = pltpu.make_async_copy(feed.at[0, 0], rows(Y1, 40, 32, (1,)), lsem.at[0])
    fed2 = pltpu.make_async_copy(feed.at[1, 0], rows(Y3, 24, 32, (1,)), lsem.at[1])
    fed3 = pltpu.make_async_copy(feed.at[2, 0], rows(Y5, 8, 32), lsem.at[2])

    pl.semaphore_wait(barrier, expected)
    start("v0")
    start("a")
    start("v1")
    start("v2")

    @pl.when(d == depths - 1)
    def _():
        start("f1")
        fed1.start()

    @pl.when(d == depths - 2)
    def _():
        start("f2")
        fed2.start()

    for copy in loads:
        copy.wait()
    turned = TC[...].T
    for g in range(TABS):
        width = min(NY, table.shape[0] - g * NY)
        TT[g, :, 0:width] = turned[:, g * NY : g * NY + width]
    wraps = [d + k >= depths for k in range(3)]
    tick_row = [jnp.where(wraps[k], 2 * depths - 1 - d, depths - 1 - d) for k in range(3)] + [depths + 2 - d]
    for k in range(4):
        for g in range(TABS):
            line = TT[g, pl.ds(tick_row[k], 1), :]
            TW[k, g] = jnp.broadcast_to(line, (8, NY))

    total = strips * W
    middle = s * W + W // 2

    def lookup(count, lev, row, base, tick):
        tab = [TW[tick, g] for g in range(TABS)]

        def levels(j, nb):
            return lev[row, pl.ds(base + j, 8, stride=nb), :]

        return lambda j: looked_up(count // 8, levels, tab, j)

    def step(count, src, lead, off, coefs, dst, dst_lead):

        def load(c, j, nb):
            return src[(*lead, c, pl.ds(off + j, 8, stride=nb), slice(None))]

        def out(c, j, nb, value):
            dst[(*dst_lead, c, pl.ds(j, 8, stride=nb), slice(None))] = value

        layer(count, load, coefs, middle - count // 2, total, out)

    received("v0")
    received("a")
    step(ROWS[0], A, (), 0, lookup(ROWS[0], V0, 0, 0, 0), Y0, ())
    step(ROWS[1], Y0, (), 8, lookup(ROWS[1], V0, 1, 8, 0), Y1, (0,))
    received("v1")

    @pl.when(d == depths - 1)
    def _():
        received("f1")
        fed1.wait()

    last1 = jnp.where(d == depths - 1, 1, 0)
    step(ROWS[2], Y1, (last1,), 8, lookup(ROWS[2], V1, 0, 0, 1), Y2, ())
    copies["i1", 0, 0].start()
    step(ROWS[3], Y2, (), 8, lookup(ROWS[3], V1, 1, 8, 1), Y3, (0,))
    copies["i1", 1, 0].start()
    received("v2")

    @pl.when(d == depths - 2)
    def _():
        received("f2")
        fed2.wait()

    last2 = jnp.where(d == depths - 2, 1, 0)
    step(ROWS[4], Y3, (last2,), 8, lookup(ROWS[4], V2, 0, 0, 2), Y4, ())
    step(ROWS[5], Y4, (), 8, lookup(ROWS[5], V2, 1, 8, 2), Y5, ())

    @pl.when(d != depths - 3)
    def _():
        start("m")

    copies["i2", 0, 0].start()
    for name in ((0, 1, 0), (0, 1, 1), (0, 1, -1)):
        guarded(there(MSGS[("i2",) + name[1:]]), copies[("i2",) + name[1:]].start)

    @pl.when(d == depths - 3)
    def _():
        for name in ((1, 0), (1, 1), (1, -1)):
            sent(("i2",) + name)
        fed3.start()
        fed3.wait()
        start("m")

    def image(sources, fresh):
        def body(k, carry):
            for row in (0, 1):
                value = None if fresh else img[row, k]
                for source in sources[row]:
                    piece = product(*source, offs[k])
                    value = piece if value is None else value + piece
                img[row, k] = value
            return carry

        lax.fori_loop(0, img.shape[1], body, 0)

    def keep(ref, count, row, base):
        get = lookup(count, V0, row, base, 3)
        for j in range(count // 8):
            for c, value in enumerate(get(j)):
                ref[c, j] = value

    def kept(ref, count):
        return lambda j: [ref[c, j] for c in range(2 * ORDER + 2)]

    keep(C6, LAST[0], 0, 24)
    keep(C7, LAST[1], 1, 32)
    image([[(Y0, (), 48)], [(Y1, (0,), 40)]], True)
    received("i1")
    image([[(I1, (0,), 8)], [(I1, (1,), 8)]], False)
    lasts_out = [
        pltpu.make_async_copy(Y6.at[:, pl.ds(16, W + 16), :], last_out.at[0], lsem.at[7]),
        pltpu.make_async_copy(Y7.at[:, pl.ds(8, W + 16), :], last_out.at[1], lsem.at[8]),
    ]
    received("m")
    step(LAST[0], M, (), 0, kept(C6, LAST[0]), Y6, ())
    lasts_out[0].start()
    step(LAST[1], Y6, (), 8, kept(C7, LAST[1]), Y7, ())
    lasts_out[1].start()
    received("i2")

    @pl.when(s == 0)
    def _():
        I2[1, :, 0:8, :] = jnp.zeros((4, 8, NY), F32)

    @pl.when(s == strips - 1)
    def _():
        I2[1, :, 40:48, :] = jnp.zeros((4, 8, NY), F32)

    image([[(I2, (0,), 8)], [(I2, (1,), 8)]], False)
    partial_out = pltpu.make_async_copy(img, img_out, lsem.at[6])
    partial_out.start()

    partial_out.wait()
    for copy in lasts_out:
        copy.wait()

    for name in copies:
        if name[0] in ("a", "v0", "v1", "v2", "i1", "m") or name == ("i2", 0, 0):
            sent(name)

    @pl.when(d == depths - 1)
    def _():
        for shift in (1, -1):
            sent(("f1", shift))

    @pl.when(d == depths - 2)
    def _():
        for shift in (1, -1):
            sent(("f2", shift))

    @pl.when(d != depths - 3)
    def _():
        for name in ((1, 0), (1, 1), (1, -1)):
            sent(("i2",) + name)


def solution(mesh):
    depths, strips = mesh.shape["depth"], mesh.shape["strip"]

    def per_device(arrivals, feed, velocity_index, offsets, coef_table):
        hbm = pl.BlockSpec(memory_space=pltpu.HBM)
        smem = pl.BlockSpec(memory_space=pltpu.SMEM)
        field = lambda n, *lead: pltpu.VMEM((*lead, 4, n, NY), F32)
        level = lambda n: pltpu.VMEM((2, n, NY), jnp.int32)
        noff = offsets.shape[0]
        columns = jnp.transpose(coef_table, (1, 2, 3, 4, 0)).reshape(-1, coef_table.shape[0])
        partial, last = pl.pallas_call(
            functools.partial(kernel, depths, strips),
            out_shape=(
                jax.ShapeDtypeStruct((2, noff, W, NY), F32),
                jax.ShapeDtypeStruct((2, 4, W + 16, NY), F32),
            ),
            in_specs=[hbm, hbm, smem, hbm, hbm],
            out_specs=(hbm, hbm),
            scratch_shapes=[
                pltpu.VMEM((2, noff, W, NY), F32),
                field(128), level(128), level(96), level(64),
                field(128), field(112, 2), field(96), field(80, 2), field(64), field(48), field(80), field(64),
                field(80), field(48, 2), field(48, 2),
                pltpu.VMEM(columns.shape, F32),
                pltpu.VMEM((TABS, coef_table.shape[0], NY), F32),
                pltpu.VMEM((4, TABS, 8, NY), F32),
                pltpu.VMEM((2 * ORDER + 2, LAST[0] // 8, 8, NY), F32),
                pltpu.VMEM((2 * ORDER + 2, LAST[1] // 8, 8, NY), F32),
                pltpu.SemaphoreType.DMA((len(MSGS),)),
                pltpu.SemaphoreType.DMA((len(MSGS),)),
                pltpu.SemaphoreType.DMA((9,)),
            ],
            compiler_params=pltpu.CompilerParams(collective_id=0, has_side_effects=True, vmem_limit_bytes=60 * 2**20),
            name="relay",
        )(arrivals, velocity_index, offsets, feed, columns)
        return pl.pallas_call(
            finish,
            out_shape=(
                jax.ShapeDtypeStruct((2, noff, W, NY), F32),
                jax.ShapeDtypeStruct((1, 1, 4, W, NY), F32),
            ),
            in_specs=[hbm, hbm, smem],
            out_specs=(hbm, hbm),
            scratch_shapes=[
                pltpu.VMEM((2, noff, W, NY), F32),
                pltpu.VMEM((2, 4, W + 16, NY), F32),
                pltpu.SemaphoreType.DMA((7,)),
            ],
            compiler_params=pltpu.CompilerParams(vmem_limit_bytes=60 * 2**20),
            name="finish",
        )(partial, last, offsets)

    return jax.shard_map(
        per_device,
        mesh=mesh,
        in_specs=(
            P("depth", None, None, "strip", None),
            P(None, None, None, "strip", None),
            P("depth", "strip", None),
            P(),
            P(),
        ),
        out_specs=(P("depth", None, "strip", None), P("depth", None, None, "strip", None)),
        check_vma=False,
    )
```

```python
import functools

import jax
import jax.numpy as jnp
from jax import lax
from jax.experimental import pallas as pl
from jax.experimental.pallas import tpu as pltpu
from jax.sharding import PartitionSpec as P

MESH = pl.DeviceIdType.MESH
ORDER = 8
W = 32
PARTS = 4
NY = 128
LEVELS = 32
TABS = (2 * (ORDER + 1) * LEVELS + NY - 1) // NY
F32 = jnp.float32

ROWS = (128, 112, 96, 80, 64, 48)
LAST = (80, 64)

MSGS = {}
for _s in (1, -1, 2, -2):
    MSGS["a", _s] = (0, _s)
    MSGS["v0", _s] = (0, _s)
for _s in (0, 1, -1):
    MSGS["v1", _s] = (-1, _s)
    MSGS["v2", _s] = (-2, _s)
    MSGS["m", _s] = (3, _s)
for _s in (1, -1):
    MSGS["f1", _s] = (0, _s)
    MSGS["f2", _s] = (0, _s)
    MSGS["i2", 1, _s] = (2, _s)
for _l in (0, 1):
    MSGS["i1", _l, 0] = (1, 0)
    MSGS["i2", _l, 0] = (2, 0)
INDEX = {name: i for i, name in enumerate(MSGS)}
PEERS = sorted(set(MSGS.values()))


def looked_up(nb, lev, tab, j):
    idx = lev(j, nb)
    idx = [idx + LEVELS * m for m in range(4)]
    return [jnp.take_along_axis(tab[c // 4], idx[c % 4], axis=1) for c in range(2 * ORDER + 2)]


def layer(rows, load, coefs, top, total, out):
    nb = rows // 8
    lanes = lax.broadcasted_iota(jnp.int32, (8, NY), 1)
    first, final = lanes == 0, lanes == NY - 1
    blocks = lax.broadcasted_iota(jnp.int32, (8, NY), 0) * nb + top
    inside = [(blocks + j >= 0) & (blocks + j < total) for j in range(nb)]
    quarter = [jnp.where(inside[j], 0.25, 0.0) for j in range(nb)]
    comps = range(4)
    t = [[jnp.where(inside[j], load(c, j, nb), 0.0) for j in range(nb)] for c in comps]
    hist = [t]
    p = None
    for n in range(1, ORDER + 1):
        new_t, new_p = [], []
        for c in comps:
            u = t[c]
            up = pltpu.roll(u[nb - 1], 1, 0)
            down = pltpu.roll(u[0], 7, 0)
            s = [u[j] + u[j + 1] for j in range(nb - 1)]
            tl, ql = [], []
            for j in range(nb):
                a = s[j - 1] if j else up + u[0]
                b = s[j] if j + 1 < nb else u[nb - 1] + down
                v = a + b
                sides = jnp.where(first, 0.0, pltpu.roll(v, 1, 1)) + jnp.where(
                    final, 0.0, pltpu.roll(v, NY - 1, 1)
                )
                q = (v + v) + sides
                if n == 1:
                    r = q * (quarter[j] * 0.5)
                else:
                    r = q * quarter[j] - p[c][j]
                ql.append(r)
                tl.append(r - u[j])
            new_t.append(tl)
            new_p.append(ql)
        t, p = new_t, new_p
        hist.append(t)
    for j in range(nb):
        chosen = coefs(j)
        acc = [None] * 4
        for n in range(ORDER + 1):
            cr, ci = chosen[2 * n], chosen[2 * n + 1]
            sr, si, rr, ri = [hist[n][c][j] for c in comps]
            new = [
                cr * sr - ci * si,
                cr * si + ci * sr,
                cr * rr + ci * ri,
                cr * ri - ci * rr,
            ]
            acc = [new[c] if n == 0 else acc[c] + new[c] for c in comps]
        for c in comps:
            out(c, j, nb, acc[c])


def product(ref, lead, at, h):
    low = [ref[(*lead, c, pl.ds(at - h, W), slice(None))] for c in (0, 1)]
    high = [ref[(*lead, c, pl.ds(at + h, W), slice(None))] for c in (2, 3)]
    return low[0] * high[0] + low[1] * high[1]


def finish(partial, last, second, offs, image, outflow, out, fields, sem):
    loads = {}
    for row in (1, 0):
        loads["last", row] = (last.at[row], fields.at[0, row])
    for row in (0, 1):
        loads["second", row] = (second.at[row], fields.at[1, row])
        for part in range(PARTS):
            some = pl.ds(part * out.shape[1] // PARTS, out.shape[1] // PARTS)
            loads[row, part] = (partial.at[row, some], out.at[row, some])
    loads = {name: pltpu.make_async_copy(*ends, sem.at[i]) for i, (name, ends) in enumerate(loads.items())}
    for copy in loads.values():
        copy.start()
    loads["last", 1].wait()
    stores = [pltpu.make_async_copy(fields.at[0, 1, :, pl.ds(8, W), :], outflow.at[0, 0], sem.at[len(loads)])]
    stores[0].start()
    loads["last", 0].wait()
    for row in (0, 1):
        loads["second", row].wait()
        for part in range(PARTS):
            loads[row, part].wait()
            first, count = part * out.shape[1] // PARTS, out.shape[1] // PARTS
            for k in range(first, first + count):
                h = offs[k]
                out[row, k] = out[row, k] + product(fields, (0, row), 8, h) + product(fields, (1, row), 8, h)
            some = pl.ds(first, count)
            stores.append(pltpu.make_async_copy(out.at[row, some], image.at[row, some], sem.at[len(loads) + len(stores)]))
            stores[-1].start()
    for copy in stores:
        copy.wait()


def kernel(depths, strips, arr, vel, offs, feed, table, img_out, last_out, second, img, A, V0, V1, V2, Y0, Y1, Y2, Y3, Y4, Y5, Y6, Y7, M, I1, I2, TC, TT, TW, C6, C7, ssem, rsem, lsem):
    d = lax.axis_index("depth")
    s = lax.axis_index("strip")

    def peer(shift):
        return (
            lax.rem(d + shift[0] + depths, depths),
            s + shift[1],
        )

    def there(shift, sign=1):
        if shift[1] == 0:
            return None
        at = s + sign * shift[1]
        return (at >= 0) & (at < strips)

    def guarded(condition, action):
        if condition is None:
            action()
        else:
            pl.when(condition)(action)

    loads = [
        pltpu.make_async_copy(table, TC, lsem.at[3]),
        pltpu.make_async_copy(arr.at[0, 0], A.at[:, pl.ds(48, 32), :], lsem.at[4]),
        pltpu.make_async_copy(vel, V0.at[:, pl.ds(48, 32), :], lsem.at[5]),
    ]
    for copy in loads:
        copy.start()

    @pl.when(s < 2)
    def _():
        V0[:, 0:48, :] = jnp.zeros((2, 48, NY), jnp.int32)
        V1[:, 0:32, :] = jnp.zeros((2, 32, NY), jnp.int32)
        V2[:, 0:16, :] = jnp.zeros((2, 16, NY), jnp.int32)

    @pl.when(s >= strips - 2)
    def _():
        V0[:, 80:128, :] = jnp.zeros((2, 48, NY), jnp.int32)
        V1[:, 64:96, :] = jnp.zeros((2, 32, NY), jnp.int32)
        V2[:, 48:64, :] = jnp.zeros((2, 16, NY), jnp.int32)

    barrier = pltpu.get_barrier_semaphore()
    expected = 0
    for shift in PEERS:
        def greet(shift=shift):
            pl.semaphore_signal(barrier, inc=1, device_id=peer((-shift[0], -shift[1])), device_id_type=MESH)

        guarded(there(shift, -1), greet)
        expected = expected + (1 if shift[1] == 0 else jnp.where(there(shift), 1, 0))

    def send(name, src, dst):
        i = INDEX[name]
        return pltpu.make_async_remote_copy(
            src_ref=src, dst_ref=dst, send_sem=ssem.at[i], recv_sem=rsem.at[i],
            device_id=peer(MSGS[name]), device_id_type=MESH,
        )

    def rows(ref, start, count, lead=()):
        return ref.at[(*lead, slice(None), pl.ds(start, count), slice(None))]

    own = arr.at[0, 0]
    lead1, lead2 = A.shape[1] // 2 - W // 2, V2.shape[1] // 2 - W // 2
    sends = {}
    sends["v0", 1] = (vel, rows(V0, 16, 32))
    sends["v0", -1] = (vel, rows(V0, 80, 32))
    sends["v0", 2] = (rows(vel, 16, 16), rows(V0, 0, 16))
    sends["v0", -2] = (rows(vel, 0, 16), rows(V0, 112, 16))
    sends["a", 1] = (own, rows(A, 16, 32))
    sends["a", -1] = (own, rows(A, 80, 32))
    sends["a", 2] = (rows(arr, 16, 16, (0, 0)), rows(A, 0, 16))
    sends["a", -2] = (rows(arr, 0, 16, (0, 0)), rows(A, 112, 16))
    sends["v1", 0] = (vel, rows(V1, 32, 32))
    sends["v1", 1] = (vel, rows(V1, 0, 32))
    sends["v1", -1] = (vel, rows(V1, 64, 32))
    sends["v2", 0] = (vel, rows(V2, 16, 32))
    sends["v2", 1] = (rows(vel, 16, 16), rows(V2, 0, 16))
    sends["v2", -1] = (rows(vel, 0, 16), rows(V2, 48, 16))
    for layer_ in (0, 1):
        sends["i1", layer_, 0] = (rows((Y2, Y3)[layer_], (24, 16)[layer_], 48, () if layer_ == 0 else (0,)), I1.at[layer_])
    sends["i2", 0, 0] = (rows(Y4, 8, 48), I2.at[0])
    sends["i2", 1, 0] = (rows(Y5, 8, 32), rows(I2, 8, 32, (1,)))
    sends["i2", 1, 1] = (rows(Y5, 32, 8), rows(I2, 0, 8, (1,)))
    sends["i2", 1, -1] = (rows(Y5, 8, 8), rows(I2, 40, 8, (1,)))
    moved = {0: (8, 32, 24), 1: (16, 24, 0), -1: (8, 24, 56)}
    for shift, (start, count, to) in moved.items():
        sends["m", shift] = (rows(Y5, start, count), rows(M, to, count))
    for shift, to in ((1, 8), (-1, 72)):
        sends["f1", shift] = (feed.at[0, 0], rows(Y1, to, 32, (1,)))
    sends["f2", 1] = (rows(feed, 16, 16, (1, 0)), rows(Y3, 8, 16, (1,)))
    sends["f2", -1] = (rows(feed, 0, 16, (1, 0)), rows(Y3, 56, 16, (1,)))
    copies = {name: send(name, *ends) for name, ends in sends.items()}

    def start(kind):
        for name in copies:
            if name[0] == kind:
                guarded(there(MSGS[name]), copies[name].start)

    def received(*kind):
        for name in copies:
            if name[: len(kind)] == kind:
                guarded(there(MSGS[name], -1), copies[name].wait_recv)

    def sent(name):
        guarded(there(MSGS[name]), copies[name].wait_send)

    fed1 = pltpu.make_async_copy(feed.at[0, 0], rows(Y1, 40, 32, (1,)), lsem.at[0])
    fed2 = pltpu.make_async_copy(feed.at[1, 0], rows(Y3, 24, 32, (1,)), lsem.at[1])
    entering = {}
    for shift, (at, count, to) in moved.items():
        entering[shift] = send(("m", shift), rows(feed, at - 8, count, (2, 0)), rows(M, to, count))

    pl.semaphore_wait(barrier, expected)
    start("v0")
    start("a")
    start("v1")
    start("v2")

    @pl.when(d == depths - 1)
    def _():
        start("f1")
        fed1.start()

    @pl.when(d == depths - 2)
    def _():
        start("f2")
        fed2.start()

    @pl.when(d == depths - 3)
    def _():
        for shift, copy in entering.items():
            guarded(there(MSGS["m", shift]), copy.start)

    for copy in loads:
        copy.wait()
    turned = TC[...].T
    for g in range(TABS):
        width = min(NY, table.shape[0] - g * NY)
        TT[g, :, 0:width] = turned[:, g * NY : g * NY + width]
    wraps = [d + k >= depths for k in range(3)]
    tick_row = [jnp.where(wraps[k], 2 * depths - 1 - d, depths - 1 - d) for k in range(3)] + [depths + 2 - d]
    for k in range(4):
        for g in range(TABS):
            line = TT[g, pl.ds(tick_row[k], 1), :]
            TW[k, g] = jnp.broadcast_to(line, (8, NY))

    total = strips * W
    middle = s * W + W // 2

    def lookup(count, lev, row, base, tick):
        tab = [TW[tick, g] for g in range(TABS)]

        def levels(j, nb):
            return lev[row, pl.ds(base + j, 8, stride=nb), :]

        return lambda j: looked_up(count // 8, levels, tab, j)

    def step(count, src, lead, off, coefs, dst, dst_lead):

        def load(c, j, nb):
            return src[(*lead, c, pl.ds(off + j, 8, stride=nb), slice(None))]

        def out(c, j, nb, value):
            dst[(*dst_lead, c, pl.ds(j, 8, stride=nb), slice(None))] = value

        layer(count, load, coefs, middle - count // 2, total, out)

    received("v0")
    received("a")
    step(ROWS[0], A, (), 0, lookup(ROWS[0], V0, 0, 0, 0), Y0, ())
    step(ROWS[1], Y0, (), 8, lookup(ROWS[1], V0, 1, 8, 0), Y1, (0,))
    received("v1")

    @pl.when(d == depths - 1)
    def _():
        received("f1")
        fed1.wait()

    last1 = jnp.where(d == depths - 1, 1, 0)
    step(ROWS[2], Y1, (last1,), 8, lookup(ROWS[2], V1, 0, 0, 1), Y2, ())
    copies["i1", 0, 0].start()
    step(ROWS[3], Y2, (), 8, lookup(ROWS[3], V1, 1, 8, 1), Y3, (0,))
    copies["i1", 1, 0].start()
    received("v2")

    @pl.when(d == depths - 2)
    def _():
        received("f2")
        fed2.wait()

    last2 = jnp.where(d == depths - 2, 1, 0)
    step(ROWS[4], Y3, (last2,), 8, lookup(ROWS[4], V2, 0, 0, 2), Y4, ())
    step(ROWS[5], Y4, (), 8, lookup(ROWS[5], V2, 1, 8, 2), Y5, ())

    @pl.when(d != depths - 3)
    def _():
        start("m")

    start("i2")

    def image(sources, fresh):
        def body(k, carry):
            for row in (0, 1):
                value = None if fresh else img[row, k]
                for source in sources[row]:
                    piece = product(*source, offs[k])
                    value = piece if value is None else value + piece
                img[row, k] = value
            return carry

        lax.fori_loop(0, img.shape[1], body, 0)

    def keep(ref, count, row, base):
        get = lookup(count, V0, row, base, 3)
        for j in range(count // 8):
            for c, value in enumerate(get(j)):
                ref[c, j] = value

    def kept(ref, count):
        return lambda j: [ref[c, j] for c in range(2 * ORDER + 2)]

    keep(C6, LAST[0], 0, 24)
    keep(C7, LAST[1], 1, 32)
    image([[(Y0, (), 48)], [(Y1, (0,), 40)]], True)
    received("i1")
    image([[(I1, (0,), 8)], [(I1, (1,), 8)]], False)
    partial_out = pltpu.make_async_copy(img, img_out, lsem.at[6])
    partial_out.start()
    lasts_out = [
        pltpu.make_async_copy(Y6.at[:, pl.ds(16, W + 16), :], last_out.at[0], lsem.at[7]),
        pltpu.make_async_copy(Y7.at[:, pl.ds(8, W + 16), :], last_out.at[1], lsem.at[8]),
    ]
    received("m")
    step(LAST[0], M, (), 0, kept(C6, LAST[0]), Y6, ())
    lasts_out[0].start()
    step(LAST[1], Y6, (), 8, kept(C7, LAST[1]), Y7, ())
    lasts_out[1].start()
    received("i2")

    @pl.when(s == 0)
    def _():
        I2[1, :, 0:8, :] = jnp.zeros((4, 8, NY), F32)

    @pl.when(s == strips - 1)
    def _():
        I2[1, :, 40:48, :] = jnp.zeros((4, 8, NY), F32)

    second_out = pltpu.make_async_copy(I2, second, lsem.at[2])
    second_out.start()

    partial_out.wait()
    second_out.wait()
    for copy in lasts_out:
        copy.wait()

    for name in copies:
        if name[0] in ("a", "v0", "v1", "v2", "i1", "i2", "m"):
            sent(name)

    @pl.when(d == depths - 1)
    def _():
        for shift in (1, -1):
            sent(("f1", shift))

    @pl.when(d == depths - 2)
    def _():
        for shift in (1, -1):
            sent(("f2", shift))


def solution(mesh):
    depths, strips = mesh.shape["depth"], mesh.shape["strip"]

    def per_device(arrivals, feed, velocity_index, offsets, coef_table):
        hbm = pl.BlockSpec(memory_space=pltpu.HBM)
        smem = pl.BlockSpec(memory_space=pltpu.SMEM)
        field = lambda n, *lead: pltpu.VMEM((*lead, 4, n, NY), F32)
        level = lambda n: pltpu.VMEM((2, n, NY), jnp.int32)
        noff = offsets.shape[0]
        columns = jnp.transpose(coef_table, (1, 2, 3, 4, 0)).reshape(-1, coef_table.shape[0])
        partial, last, second = pl.pallas_call(
            functools.partial(kernel, depths, strips),
            out_shape=(
                jax.ShapeDtypeStruct((2, noff, W, NY), F32),
                jax.ShapeDtypeStruct((2, 4, W + 16, NY), F32),
                jax.ShapeDtypeStruct((2, 4, W + 16, NY), F32),
            ),
            in_specs=[hbm, hbm, smem, hbm, hbm],
            out_specs=(hbm, hbm, hbm),
            scratch_shapes=[
                pltpu.VMEM((2, noff, W, NY), F32),
                field(128), level(128), level(96), level(64),
                field(128), field(112, 2), field(96), field(80, 2), field(64), field(48), field(80), field(64),
                field(80), field(48, 2), field(48, 2),
                pltpu.VMEM(columns.shape, F32),
                pltpu.VMEM((TABS, coef_table.shape[0], NY), F32),
                pltpu.VMEM((4, TABS, 8, NY), F32),
                pltpu.VMEM((2 * ORDER + 2, LAST[0] // 8, 8, NY), F32),
                pltpu.VMEM((2 * ORDER + 2, LAST[1] // 8, 8, NY), F32),
                pltpu.SemaphoreType.DMA((len(MSGS),)),
                pltpu.SemaphoreType.DMA((len(MSGS),)),
                pltpu.SemaphoreType.DMA((9,)),
            ],
            compiler_params=pltpu.CompilerParams(collective_id=0, has_side_effects=True, vmem_limit_bytes=60 * 2**20),
            name="relay",
        )(arrivals, velocity_index, offsets, feed, columns)
        return pl.pallas_call(
            finish,
            out_shape=(
                jax.ShapeDtypeStruct((2, noff, W, NY), F32),
                jax.ShapeDtypeStruct((1, 1, 4, W, NY), F32),
            ),
            in_specs=[hbm, hbm, hbm, smem],
            out_specs=(hbm, hbm),
            scratch_shapes=[
                pltpu.VMEM((2, noff, W, NY), F32),
                pltpu.VMEM((2, 2, 4, W + 16, NY), F32),
                pltpu.SemaphoreType.DMA((4 * PARTS + 5,)),
            ],
            compiler_params=pltpu.CompilerParams(vmem_limit_bytes=60 * 2**20),
            name="finish",
        )(partial, last, second, offsets)

    return jax.shard_map(
        per_device,
        mesh=mesh,
        in_specs=(
            P("depth", None, None, "strip", None),
            P(None, None, None, "strip", None),
            P("depth", "strip", None),
            P(),
            P(),
        ),
        out_specs=(P("depth", None, "strip", None), P("depth", None, None, "strip", None)),
        check_vma=False,
    )
```

```python
import functools

import jax
import jax.numpy as jnp
from jax import lax
from jax.experimental import pallas as pl
from jax.experimental.pallas import tpu as pltpu
from jax.sharding import PartitionSpec as P

MESH = pl.DeviceIdType.MESH
ORDER = 8
W = 32
PARTS = 4
NY = 128
LEVELS = 32
TABS = (2 * (ORDER + 1) * LEVELS + NY - 1) // NY
F32 = jnp.float32

ROWS = (128, 112, 96, 80, 64, 48)
LAST = (80, 64)

MSGS = {}
for _s in (1, -1, 2, -2):
    MSGS["a", _s] = (0, _s)
    MSGS["v0", _s] = (0, _s)
for _s in (0, 1, -1):
    MSGS["v1", _s] = (-1, _s)
    MSGS["v2", _s] = (-2, _s)
    MSGS["m", _s] = (3, _s)
for _s in (1, -1):
    MSGS["f1", _s] = (0, _s)
    MSGS["f2", _s] = (0, _s)
    MSGS["i2", 1, _s] = (2, _s)
    MSGS["e1", _s] = (0, _s)
    MSGS["e2", _s] = (0, _s)
for _l in (0, 1):
    MSGS["i1", _l, 0] = (1, 0)
    MSGS["i2", _l, 0] = (2, 0)
INDEX = {name: i for i, name in enumerate(MSGS)}
PEERS = sorted(set(MSGS.values()))


def looked_up(nb, lev, tab, j):
    idx = lev(j, nb)
    idx = [idx + LEVELS * m for m in range(4)]
    return [jnp.take_along_axis(tab[c // 4], idx[c % 4], axis=1) for c in range(2 * ORDER + 2)]


def layer(rows, load, coefs, top, total, out):
    nb = rows // 8
    lanes = lax.broadcasted_iota(jnp.int32, (8, NY), 1)
    first, final = lanes == 0, lanes == NY - 1
    blocks = lax.broadcasted_iota(jnp.int32, (8, NY), 0) * nb + top
    inside = [(blocks + j >= 0) & (blocks + j < total) for j in range(nb)]
    quarter = [jnp.where(inside[j], 0.25, 0.0) for j in range(nb)]
    comps = range(4)
    t = [[jnp.where(inside[j], load(c, j, nb), 0.0) for j in range(nb)] for c in comps]
    hist = [t]
    p = None
    for n in range(1, ORDER + 1):
        new_t, new_p = [], []
        for c in comps:
            u = t[c]
            up = pltpu.roll(u[nb - 1], 1, 0)
            down = pltpu.roll(u[0], 7, 0)
            s = [u[j] + u[j + 1] for j in range(nb - 1)]
            tl, ql = [], []
            for j in range(nb):
                a = s[j - 1] if j else up + u[0]
                b = s[j] if j + 1 < nb else u[nb - 1] + down
                v = a + b
                sides = jnp.where(first, 0.0, pltpu.roll(v, 1, 1)) + jnp.where(
                    final, 0.0, pltpu.roll(v, NY - 1, 1)
                )
                q = (v + v) + sides
                if n == 1:
                    r = q * (quarter[j] * 0.5)
                else:
                    r = q * quarter[j] - p[c][j]
                ql.append(r)
                tl.append(r - u[j])
            new_t.append(tl)
            new_p.append(ql)
        t, p = new_t, new_p
        hist.append(t)
    for j in range(nb):
        chosen = coefs(j)
        acc = [None] * 4
        for n in range(ORDER + 1):
            cr, ci = chosen[2 * n], chosen[2 * n + 1]
            sr, si, rr, ri = [hist[n][c][j] for c in comps]
            new = [
                cr * sr - ci * si,
                cr * si + ci * sr,
                cr * rr + ci * ri,
                cr * ri - ci * rr,
            ]
            acc = [new[c] if n == 0 else acc[c] + new[c] for c in comps]
        for c in comps:
            out(c, j, nb, acc[c])


def product(ref, lead, at, h):
    low = [ref[(*lead, c, pl.ds(at - h, W), slice(None))] for c in (0, 1)]
    high = [ref[(*lead, c, pl.ds(at + h, W), slice(None))] for c in (2, 3)]
    return low[0] * high[0] + low[1] * high[1]


def finish(partial, last, second, offs, image, outflow, out, fields, sem):
    loads = {}
    for row in (1, 0):
        loads["last", row] = (last.at[row], fields.at[0, row])
    for row in (0, 1):
        loads["second", row] = (second.at[row], fields.at[1, row])
        for part in range(PARTS):
            some = pl.ds(part * out.shape[1] // PARTS, out.shape[1] // PARTS)
            loads[row, part] = (partial.at[row, some], out.at[row, some])
    loads = {name: pltpu.make_async_copy(*ends, sem.at[i]) for i, (name, ends) in enumerate(loads.items())}
    for copy in loads.values():
        copy.start()
    loads["last", 1].wait()
    stores = [pltpu.make_async_copy(fields.at[0, 1, :, pl.ds(8, W), :], outflow.at[0, 0], sem.at[len(loads)])]
    stores[0].start()
    loads["last", 0].wait()
    for row in (0, 1):
        loads["second", row].wait()
        for part in range(PARTS):
            loads[row, part].wait()
            first, count = part * out.shape[1] // PARTS, out.shape[1] // PARTS
            for k in range(first, first + count):
                h = offs[k]
                out[row, k] = out[row, k] + product(fields, (0, row), 8, h) + product(fields, (1, row), 8, h)
            some = pl.ds(first, count)
            stores.append(pltpu.make_async_copy(out.at[row, some], image.at[row, some], sem.at[len(loads) + len(stores)]))
            stores[-1].start()
    for copy in stores:
        copy.wait()


def kernel(depths, strips, arr, vel, offs, feed, table, img_out, last_out, second, img, A, V0, V1, V2, Y0, Y1, Y2, Y3, Y4, Y5, Y6, Y7, M, I1, I2, TC, TT, TW, C6, C7, ssem, rsem, lsem):
    d = lax.axis_index("depth")
    s = lax.axis_index("strip")

    def peer(shift):
        return (
            lax.rem(d + shift[0] + depths, depths),
            s + shift[1],
        )

    def there(shift, sign=1):
        if shift[1] == 0:
            return None
        at = s + sign * shift[1]
        return (at >= 0) & (at < strips)

    def guarded(condition, action):
        if condition is None:
            action()
        else:
            pl.when(condition)(action)

    loads = [
        pltpu.make_async_copy(table, TC, lsem.at[3]),
        pltpu.make_async_copy(arr.at[0, 0], A.at[:, pl.ds(48, 32), :], lsem.at[4]),
        pltpu.make_async_copy(vel, V0.at[:, pl.ds(48, 32), :], lsem.at[5]),
    ]
    for copy in loads:
        copy.start()

    @pl.when(s < 2)
    def _():
        V0[:, 0:48, :] = jnp.zeros((2, 48, NY), jnp.int32)
        V1[:, 0:32, :] = jnp.zeros((2, 32, NY), jnp.int32)
        V2[:, 0:16, :] = jnp.zeros((2, 16, NY), jnp.int32)

    @pl.when(s >= strips - 2)
    def _():
        V0[:, 80:128, :] = jnp.zeros((2, 48, NY), jnp.int32)
        V1[:, 64:96, :] = jnp.zeros((2, 32, NY), jnp.int32)
        V2[:, 48:64, :] = jnp.zeros((2, 16, NY), jnp.int32)

    for end, at in ((0, 0), (strips - 1, 40)):
        @pl.when(s == end)
        def _(at=at):
            for ref in (I1, I2):
                ref[:, :, at : at + 8, :] = jnp.zeros((2, 4, 8, NY), F32)

    barrier = pltpu.get_barrier_semaphore()
    expected = 0
    for shift in PEERS:
        def greet(shift=shift):
            pl.semaphore_signal(barrier, inc=1, device_id=peer((-shift[0], -shift[1])), device_id_type=MESH)

        guarded(there(shift, -1), greet)
        expected = expected + (1 if shift[1] == 0 else jnp.where(there(shift), 1, 0))

    def send(name, src, dst):
        i = INDEX[name]
        return pltpu.make_async_remote_copy(
            src_ref=src, dst_ref=dst, send_sem=ssem.at[i], recv_sem=rsem.at[i],
            device_id=peer(MSGS[name]), device_id_type=MESH,
        )

    def rows(ref, start, count, lead=()):
        return ref.at[(*lead, slice(None), pl.ds(start, count), slice(None))]

    own = arr.at[0, 0]
    lead1, lead2 = A.shape[1] // 2 - W // 2, V2.shape[1] // 2 - W // 2
    sends = {}
    sends["v0", 1] = (vel, rows(V0, 16, 32))
    sends["v0", -1] = (vel, rows(V0, 80, 32))
    sends["v0", 2] = (rows(vel, 16, 16), rows(V0, 0, 16))
    sends["v0", -2] = (rows(vel, 0, 16), rows(V0, 112, 16))
    sends["a", 1] = (own, rows(A, 16, 32))
    sends["a", -1] = (own, rows(A, 80, 32))
    sends["a", 2] = (rows(arr, 16, 16, (0, 0)), rows(A, 0, 16))
    sends["a", -2] = (rows(arr, 0, 16, (0, 0)), rows(A, 112, 16))
    sends["v1", 0] = (vel, rows(V1, 32, 32))
    sends["v1", 1] = (vel, rows(V1, 0, 32))
    sends["v1", -1] = (vel, rows(V1, 64, 32))
    sends["v2", 0] = (vel, rows(V2, 16, 32))
    sends["v2", 1] = (rows(vel, 16, 16), rows(V2, 0, 16))
    sends["v2", -1] = (rows(vel, 0, 16), rows(V2, 48, 16))
    for layer_ in (0, 1):
        sends["i1", layer_, 0] = (
            rows((Y2, Y3)[layer_], (32, 24)[layer_], 32, () if layer_ == 0 else (0,)),
            rows(I1, 8, 32, (layer_,)),
        )
    sends["i2", 0, 0] = (rows(Y4, 16, 32), rows(I2, 8, 32, (0,)))
    for shift, at, to in ((1, 32, 0), (-1, 8, 40)):
        sends["e1", shift] = [I1.at[:, :, pl.ds(row, 8), :] for row in (at, to)]
        sends["e2", shift] = [rows(I2, row, 8, (0,)) for row in (at, to)]
    sends["i2", 1, 0] = (rows(Y5, 8, 32), rows(I2, 8, 32, (1,)))
    sends["i2", 1, 1] = (rows(Y5, 32, 8), rows(I2, 0, 8, (1,)))
    sends["i2", 1, -1] = (rows(Y5, 8, 8), rows(I2, 40, 8, (1,)))
    moved = {0: (8, 32, 24), 1: (16, 24, 0), -1: (8, 24, 56)}
    for shift, (start, count, to) in moved.items():
        sends["m", shift] = (rows(Y5, start, count), rows(M, to, count))
    for shift, to in ((1, 8), (-1, 72)):
        sends["f1", shift] = (feed.at[0, 0], rows(Y1, to, 32, (1,)))
    sends["f2", 1] = (rows(feed, 16, 16, (1, 0)), rows(Y3, 8, 16, (1,)))
    sends["f2", -1] = (rows(feed, 0, 16, (1, 0)), rows(Y3, 56, 16, (1,)))
    copies = {name: send(name, *ends) for name, ends in sends.items()}

    def start(kind):
        for name in copies:
            if name[0] == kind:
                guarded(there(MSGS[name]), copies[name].start)

    def received(*kind):
        for name in copies:
            if name[: len(kind)] == kind:
                guarded(there(MSGS[name], -1), copies[name].wait_recv)

    def sent(name):
        guarded(there(MSGS[name]), copies[name].wait_send)

    fed1 = pltpu.make_async_copy(feed.at[0, 0], rows(Y1, 40, 32, (1,)), lsem.at[0])
    fed2 = pltpu.make_async_copy(feed.at[1, 0], rows(Y3, 24, 32, (1,)), lsem.at[1])
    entering = {}
    for shift, (at, count, to) in moved.items():
        entering[shift] = send(("m", shift), rows(feed, at - 8, count, (2, 0)), rows(M, to, count))

    pl.semaphore_wait(barrier, expected)
    start("v0")
    start("a")
    start("v1")
    start("v2")

    @pl.when(d == depths - 1)
    def _():
        start("f1")
        fed1.start()

    @pl.when(d == depths - 2)
    def _():
        start("f2")
        fed2.start()

    @pl.when(d == depths - 3)
    def _():
        for shift, copy in entering.items():
            guarded(there(MSGS["m", shift]), copy.start)

    for copy in loads:
        copy.wait()
    turned = TC[...].T
    for g in range(TABS):
        width = min(NY, table.shape[0] - g * NY)
        TT[g, :, 0:width] = turned[:, g * NY : g * NY + width]
    wraps = [d + k >= depths for k in range(3)]
    tick_row = [jnp.where(wraps[k], 2 * depths - 1 - d, depths - 1 - d) for k in range(3)] + [depths + 2 - d]
    for k in range(4):
        for g in range(TABS):
            line = TT[g, pl.ds(tick_row[k], 1), :]
            TW[k, g] = jnp.broadcast_to(line, (8, NY))

    total = strips * W
    middle = s * W + W // 2

    def lookup(count, lev, row, base, tick):
        tab = [TW[tick, g] for g in range(TABS)]

        def levels(j, nb):
            return lev[row, pl.ds(base + j, 8, stride=nb), :]

        return lambda j: looked_up(count // 8, levels, tab, j)

    def step(count, src, lead, off, coefs, dst, dst_lead):

        def load(c, j, nb):
            return src[(*lead, c, pl.ds(off + j, 8, stride=nb), slice(None))]

        def out(c, j, nb, value):
            dst[(*dst_lead, c, pl.ds(j, 8, stride=nb), slice(None))] = value

        layer(count, load, coefs, middle - count // 2, total, out)

    received("v0")
    received("a")
    step(ROWS[0], A, (), 0, lookup(ROWS[0], V0, 0, 0, 0), Y0, ())
    step(ROWS[1], Y0, (), 8, lookup(ROWS[1], V0, 1, 8, 0), Y1, (0,))
    received("v1")

    @pl.when(d == depths - 1)
    def _():
        received("f1")
        fed1.wait()

    last1 = jnp.where(d == depths - 1, 1, 0)
    step(ROWS[2], Y1, (last1,), 8, lookup(ROWS[2], V1, 0, 0, 1), Y2, ())
    copies["i1", 0, 0].start()
    step(ROWS[3], Y2, (), 8, lookup(ROWS[3], V1, 1, 8, 1), Y3, (0,))
    copies["i1", 1, 0].start()
    received("v2")

    @pl.when(d == depths - 2)
    def _():
        received("f2")
        fed2.wait()

    last2 = jnp.where(d == depths - 2, 1, 0)
    step(ROWS[4], Y3, (last2,), 8, lookup(ROWS[4], V2, 0, 0, 2), Y4, ())
    step(ROWS[5], Y4, (), 8, lookup(ROWS[5], V2, 1, 8, 2), Y5, ())

    @pl.when(d != depths - 3)
    def _():
        start("m")

    start("i2")

    def image(sources, fresh):
        def body(k, carry):
            for row in (0, 1):
                value = None if fresh else img[row, k]
                for source in sources[row]:
                    piece = product(*source, offs[k])
                    value = piece if value is None else value + piece
                img[row, k] = value
            return carry

        lax.fori_loop(0, img.shape[1], body, 0)

    def keep(ref, count, row, base):
        get = lookup(count, V0, row, base, 3)
        for j in range(count // 8):
            for c, value in enumerate(get(j)):
                ref[c, j] = value

    def kept(ref, count):
        return lambda j: [ref[c, j] for c in range(2 * ORDER + 2)]

    received("i1")
    start("e1")
    keep(C6, LAST[0], 0, 24)
    keep(C7, LAST[1], 1, 32)
    image([[(Y0, (), 48)], [(Y1, (0,), 40)]], True)
    received("e1")
    image([[(I1, (0,), 8)], [(I1, (1,), 8)]], False)
    partial_out = pltpu.make_async_copy(img, img_out, lsem.at[6])
    partial_out.start()
    lasts_out = [
        pltpu.make_async_copy(Y6.at[:, pl.ds(16, W + 16), :], last_out.at[0], lsem.at[7]),
        pltpu.make_async_copy(Y7.at[:, pl.ds(8, W + 16), :], last_out.at[1], lsem.at[8]),
    ]
    received("m")
    step(LAST[0], M, (), 0, kept(C6, LAST[0]), Y6, ())
    lasts_out[0].start()
    received("i2", 0)
    start("e2")
    step(LAST[1], Y6, (), 8, kept(C7, LAST[1]), Y7, ())
    lasts_out[1].start()
    received("i2", 1)
    received("e2")

    second_out = pltpu.make_async_copy(I2, second, lsem.at[2])
    second_out.start()

    partial_out.wait()
    second_out.wait()
    for copy in lasts_out:
        copy.wait()

    for name in copies:
        if name[0] in ("a", "v0", "v1", "v2", "i1", "i2", "e1", "e2", "m"):
            sent(name)

    @pl.when(d == depths - 1)
    def _():
        for shift in (1, -1):
            sent(("f1", shift))

    @pl.when(d == depths - 2)
    def _():
        for shift in (1, -1):
            sent(("f2", shift))


def solution(mesh):
    depths, strips = mesh.shape["depth"], mesh.shape["strip"]

    def per_device(arrivals, feed, velocity_index, offsets, coef_table):
        hbm = pl.BlockSpec(memory_space=pltpu.HBM)
        smem = pl.BlockSpec(memory_space=pltpu.SMEM)
        field = lambda n, *lead: pltpu.VMEM((*lead, 4, n, NY), F32)
        level = lambda n: pltpu.VMEM((2, n, NY), jnp.int32)
        noff = offsets.shape[0]
        columns = jnp.transpose(coef_table, (1, 2, 3, 4, 0)).reshape(-1, coef_table.shape[0])
        partial, last, second = pl.pallas_call(
            functools.partial(kernel, depths, strips),
            out_shape=(
                jax.ShapeDtypeStruct((2, noff, W, NY), F32),
                jax.ShapeDtypeStruct((2, 4, W + 16, NY), F32),
                jax.ShapeDtypeStruct((2, 4, W + 16, NY), F32),
            ),
            in_specs=[hbm, hbm, smem, hbm, hbm],
            out_specs=(hbm, hbm, hbm),
            scratch_shapes=[
                pltpu.VMEM((2, noff, W, NY), F32),
                field(128), level(128), level(96), level(64),
                field(128), field(112, 2), field(96), field(80, 2), field(64), field(48), field(80), field(64),
                field(80), field(48, 2), field(48, 2),
                pltpu.VMEM(columns.shape, F32),
                pltpu.VMEM((TABS, coef_table.shape[0], NY), F32),
                pltpu.VMEM((4, TABS, 8, NY), F32),
                pltpu.VMEM((2 * ORDER + 2, LAST[0] // 8, 8, NY), F32),
                pltpu.VMEM((2 * ORDER + 2, LAST[1] // 8, 8, NY), F32),
                pltpu.SemaphoreType.DMA((len(MSGS),)),
                pltpu.SemaphoreType.DMA((len(MSGS),)),
                pltpu.SemaphoreType.DMA((9,)),
            ],
            compiler_params=pltpu.CompilerParams(collective_id=0, has_side_effects=True, vmem_limit_bytes=60 * 2**20),
            name="relay",
        )(arrivals, velocity_index, offsets, feed, columns)
        return pl.pallas_call(
            finish,
            out_shape=(
                jax.ShapeDtypeStruct((2, noff, W, NY), F32),
                jax.ShapeDtypeStruct((1, 1, 4, W, NY), F32),
            ),
            in_specs=[hbm, hbm, hbm, smem],
            out_specs=(hbm, hbm),
            scratch_shapes=[
                pltpu.VMEM((2, noff, W, NY), F32),
                pltpu.VMEM((2, 2, 4, W + 16, NY), F32),
                pltpu.SemaphoreType.DMA((4 * PARTS + 5,)),
            ],
            compiler_params=pltpu.CompilerParams(vmem_limit_bytes=60 * 2**20),
            name="finish",
        )(partial, last, second, offsets)

    return jax.shard_map(
        per_device,
        mesh=mesh,
        in_specs=(
            P("depth", None, None, "strip", None),
            P(None, None, None, "strip", None),
            P("depth", "strip", None),
            P(),
            P(),
        ),
        out_specs=(P("depth", None, "strip", None), P("depth", None, None, "strip", None)),
        check_vma=False,
    )
```

```python
import functools

import jax
import jax.numpy as jnp
from jax import lax
from jax.experimental import pallas as pl
from jax.experimental.pallas import tpu as pltpu
from jax.sharding import PartitionSpec as P

MESH = pl.DeviceIdType.MESH
ORDER = 8
W = 32
PARTS = 4
NY = 128
LEVELS = 32
TABS = (2 * (ORDER + 1) * LEVELS + NY - 1) // NY
F32 = jnp.float32

ROWS = (128, 112, 96, 80, 64, 48)
LAST = (80, 64)

MSGS = {}
for _s in (1, -1, 2, -2):
    MSGS["a", _s] = (0, _s)
    MSGS["v0", _s] = (0, _s)
for _s in (0, 1, -1):
    MSGS["v1", _s] = (-1, _s)
    MSGS["v2", _s] = (-2, _s)
    MSGS["m", _s] = (3, _s)
for _s in (1, -1):
    MSGS["f1", _s] = (0, _s)
    MSGS["f2", _s] = (0, _s)
    MSGS["i2", 1, _s] = (2, _s)
    MSGS["e1", _s] = (0, _s)
    MSGS["e2", _s] = (0, _s)
for _l in (0, 1):
    MSGS["i1", _l, 0] = (1, 0)
    MSGS["i2", _l, 0] = (2, 0)
INDEX = {name: i for i, name in enumerate(MSGS)}
PEERS = sorted(set(MSGS.values()) | {(-a, -b) for a, b in MSGS.values()})


def looked_up(nb, lev, tab, j):
    idx = lev(j, nb)
    idx = [idx + LEVELS * m for m in range(4)]
    return [jnp.take_along_axis(tab[c // 4], idx[c % 4], axis=1) for c in range(2 * ORDER + 2)]


def layer(rows, load, coefs, top, total, out):
    nb = rows // 8
    lanes = lax.broadcasted_iota(jnp.int32, (8, NY), 1)
    first, final = lanes == 0, lanes == NY - 1
    blocks = lax.broadcasted_iota(jnp.int32, (8, NY), 0) * nb + top
    inside = [(blocks + j >= 0) & (blocks + j < total) for j in range(nb)]
    quarter = [jnp.where(inside[j], 0.25, 0.0) for j in range(nb)]
    comps = range(4)
    t = [[jnp.where(inside[j], load(c, j, nb), 0.0) for j in range(nb)] for c in comps]
    hist = [t]
    p = None
    for n in range(1, ORDER + 1):
        new_t, new_p = [], []
        for c in comps:
            u = t[c]
            up = pltpu.roll(u[nb - 1], 1, 0)
            down = pltpu.roll(u[0], 7, 0)
            s = [u[j] + u[j + 1] for j in range(nb - 1)]
            tl, ql = [], []
            for j in range(nb):
                a = s[j - 1] if j else up + u[0]
                b = s[j] if j + 1 < nb else u[nb - 1] + down
                v = a + b
                sides = jnp.where(first, 0.0, pltpu.roll(v, 1, 1)) + jnp.where(
                    final, 0.0, pltpu.roll(v, NY - 1, 1)
                )
                q = (v + v) + sides
                if n == 1:
                    r = q * (quarter[j] * 0.5)
                else:
                    r = q * quarter[j] - p[c][j]
                ql.append(r)
                tl.append(r - u[j])
            new_t.append(tl)
            new_p.append(ql)
        t, p = new_t, new_p
        hist.append(t)
    for j in range(nb):
        chosen = coefs(j)
        acc = [None] * 4
        for n in range(ORDER + 1):
            cr, ci = chosen[2 * n], chosen[2 * n + 1]
            sr, si, rr, ri = [hist[n][c][j] for c in comps]
            new = [
                cr * sr - ci * si,
                cr * si + ci * sr,
                cr * rr + ci * ri,
                cr * ri - ci * rr,
            ]
            acc = [new[c] if n == 0 else acc[c] + new[c] for c in comps]
        for c in comps:
            out(c, j, nb, acc[c])


def product(ref, lead, at, h):
    low = [ref[(*lead, c, pl.ds(at - h, W), slice(None))] for c in (0, 1)]
    high = [ref[(*lead, c, pl.ds(at + h, W), slice(None))] for c in (2, 3)]
    return low[0] * high[0] + low[1] * high[1]


def finish(partial, last, second, offs, image, outflow, out, fields, sem):
    loads = {}
    for row in (1, 0):
        loads["last", row] = (last.at[row], fields.at[0, row])
    for row in (0, 1):
        loads["second", row] = (second.at[row], fields.at[1, row])
        for part in range(PARTS):
            some = pl.ds(part * out.shape[1] // PARTS, out.shape[1] // PARTS)
            loads[row, part] = (partial.at[row, some], out.at[row, some])
    loads = {name: pltpu.make_async_copy(*ends, sem.at[i]) for i, (name, ends) in enumerate(loads.items())}
    for copy in loads.values():
        copy.start()
    loads["last", 1].wait()
    stores = [pltpu.make_async_copy(fields.at[0, 1, :, pl.ds(8, W), :], outflow.at[0, 0], sem.at[len(loads)])]
    stores[0].start()
    loads["last", 0].wait()
    for row in (0, 1):
        loads["second", row].wait()
        for part in range(PARTS):
            loads[row, part].wait()
            first, count = part * out.shape[1] // PARTS, out.shape[1] // PARTS
            for k in range(first, first + count):
                h = offs[k]
                out[row, k] = out[row, k] + product(fields, (0, row), 8, h) + product(fields, (1, row), 8, h)
            some = pl.ds(first, count)
            stores.append(pltpu.make_async_copy(out.at[row, some], image.at[row, some], sem.at[len(loads) + len(stores)]))
            stores[-1].start()
    for copy in stores:
        copy.wait()


def kernel(depths, strips, arr, vel, offs, feed, table, img_out, last_out, second, img, A, V0, V1, V2, Y0, Y1, Y2, Y3, Y4, Y5, Y6, Y7, M, I1, I2, TC, TT, TW, C6, C7, ssem, rsem, lsem, ready):
    d = lax.axis_index("depth")
    s = lax.axis_index("strip")

    def peer(shift):
        return (
            lax.rem(d + shift[0] + depths, depths),
            s + shift[1],
        )

    def there(shift, sign=1):
        if shift[1] == 0:
            return None
        at = s + sign * shift[1]
        return (at >= 0) & (at < strips)

    def guarded(condition, action):
        if condition is None:
            action()
        else:
            pl.when(condition)(action)

    loads = [
        pltpu.make_async_copy(table, TC, lsem.at[3]),
        pltpu.make_async_copy(arr.at[0, 0], A.at[:, pl.ds(48, 32), :], lsem.at[4]),
        pltpu.make_async_copy(vel, V0.at[:, pl.ds(48, 32), :], lsem.at[5]),
    ]
    for copy in loads:
        copy.start()

    @pl.when(s < 2)
    def _():
        V0[:, 0:48, :] = jnp.zeros((2, 48, NY), jnp.int32)
        V1[:, 0:32, :] = jnp.zeros((2, 32, NY), jnp.int32)
        V2[:, 0:16, :] = jnp.zeros((2, 16, NY), jnp.int32)

    @pl.when(s >= strips - 2)
    def _():
        V0[:, 80:128, :] = jnp.zeros((2, 48, NY), jnp.int32)
        V1[:, 64:96, :] = jnp.zeros((2, 32, NY), jnp.int32)
        V2[:, 48:64, :] = jnp.zeros((2, 16, NY), jnp.int32)

    for end, at in ((0, 0), (strips - 1, 40)):
        @pl.when(s == end)
        def _(at=at):
            for ref in (I1, I2):
                ref[:, :, at : at + 8, :] = jnp.zeros((2, 4, 8, NY), F32)

    barrier = pltpu.get_barrier_semaphore()
    lowers, uppers = 0, 0
    answers = []
    for shift in PEERS:
        exists = there(shift)
        if shift[1]:
            upper, lower = (exists, None) if shift[1] > 0 else (None, exists)
        else:
            upper = lax.rem(d + shift[0] + depths, depths) > d
            lower = jnp.logical_not(upper)
        if upper is not None:
            def greet(shift=shift):
                pl.semaphore_signal(barrier, inc=1, device_id=peer(shift), device_id_type=MESH)

            pl.when(upper)(greet)
            uppers = uppers + jnp.where(upper, 1, 0)
        if lower is not None:
            def answer(shift=shift):
                pl.semaphore_signal(ready, inc=1, device_id=peer(shift), device_id_type=MESH)

            answers.append((lower, answer))
            lowers = lowers + jnp.where(lower, 1, 0)

    def send(name, src, dst):
        i = INDEX[name]
        return pltpu.make_async_remote_copy(
            src_ref=src, dst_ref=dst, send_sem=ssem.at[i], recv_sem=rsem.at[i],
            device_id=peer(MSGS[name]), device_id_type=MESH,
        )

    def rows(ref, start, count, lead=()):
        return ref.at[(*lead, slice(None), pl.ds(start, count), slice(None))]

    own = arr.at[0, 0]
    lead1, lead2 = A.shape[1] // 2 - W // 2, V2.shape[1] // 2 - W // 2
    sends = {}
    sends["v0", 1] = (vel, rows(V0, 16, 32))
    sends["v0", -1] = (vel, rows(V0, 80, 32))
    sends["v0", 2] = (rows(vel, 16, 16), rows(V0, 0, 16))
    sends["v0", -2] = (rows(vel, 0, 16), rows(V0, 112, 16))
    sends["a", 1] = (own, rows(A, 16, 32))
    sends["a", -1] = (own, rows(A, 80, 32))
    sends["a", 2] = (rows(arr, 16, 16, (0, 0)), rows(A, 0, 16))
    sends["a", -2] = (rows(arr, 0, 16, (0, 0)), rows(A, 112, 16))
    sends["v1", 0] = (vel, rows(V1, 32, 32))
    sends["v1", 1] = (vel, rows(V1, 0, 32))
    sends["v1", -1] = (vel, rows(V1, 64, 32))
    sends["v2", 0] = (vel, rows(V2, 16, 32))
    sends["v2", 1] = (rows(vel, 16, 16), rows(V2, 0, 16))
    sends["v2", -1] = (rows(vel, 0, 16), rows(V2, 48, 16))
    for layer_ in (0, 1):
        sends["i1", layer_, 0] = (
            rows((Y2, Y3)[layer_], (32, 24)[layer_], 32, () if layer_ == 0 else (0,)),
            rows(I1, 8, 32, (layer_,)),
        )
    sends["i2", 0, 0] = (rows(Y4, 16, 32), rows(I2, 8, 32, (0,)))
    for shift, at, to in ((1, 32, 0), (-1, 8, 40)):
        sends["e1", shift] = [I1.at[:, :, pl.ds(row, 8), :] for row in (at, to)]
        sends["e2", shift] = [rows(I2, row, 8, (0,)) for row in (at, to)]
    sends["i2", 1, 0] = (rows(Y5, 8, 32), rows(I2, 8, 32, (1,)))
    sends["i2", 1, 1] = (rows(Y5, 32, 8), rows(I2, 0, 8, (1,)))
    sends["i2", 1, -1] = (rows(Y5, 8, 8), rows(I2, 40, 8, (1,)))
    moved = {0: (8, 32, 24), 1: (16, 24, 0), -1: (8, 24, 56)}
    for shift, (start, count, to) in moved.items():
        sends["m", shift] = (rows(Y5, start, count), rows(M, to, count))
    for shift, to in ((1, 8), (-1, 72)):
        sends["f1", shift] = (feed.at[0, 0], rows(Y1, to, 32, (1,)))
    sends["f2", 1] = (rows(feed, 16, 16, (1, 0)), rows(Y3, 8, 16, (1,)))
    sends["f2", -1] = (rows(feed, 0, 16, (1, 0)), rows(Y3, 56, 16, (1,)))
    copies = {name: send(name, *ends) for name, ends in sends.items()}

    def start(kind):
        for name in copies:
            if name[0] == kind:
                guarded(there(MSGS[name]), copies[name].start)

    def received(*kind):
        for name in copies:
            if name[: len(kind)] == kind:
                guarded(there(MSGS[name], -1), copies[name].wait_recv)

    def sent(name):
        guarded(there(MSGS[name]), copies[name].wait_send)

    fed1 = pltpu.make_async_copy(feed.at[0, 0], rows(Y1, 40, 32, (1,)), lsem.at[0])
    fed2 = pltpu.make_async_copy(feed.at[1, 0], rows(Y3, 24, 32, (1,)), lsem.at[1])
    entering = {}
    for shift, (at, count, to) in moved.items():
        entering[shift] = send(("m", shift), rows(feed, at - 8, count, (2, 0)), rows(M, to, count))

    @pl.when(lowers > 0)
    def _():
        pl.semaphore_wait(barrier, lowers)

    for lower, answer in answers:
        pl.when(lower)(answer)
    downward = [name for kind in ("v0", "a", "v1", "v2") for name in copies if name[0] == kind and MSGS[name][1] < 0]
    onward = [name for kind in ("v0", "a", "v1", "v2") for name in copies if name[0] == kind and MSGS[name][1] >= 0]
    for name in downward:
        guarded(there(MSGS[name]), copies[name].start)

    @pl.when(uppers > 0)
    def _():
        pl.semaphore_wait(ready, uppers)

    for name in onward:
        guarded(there(MSGS[name]), copies[name].start)

    @pl.when(d == depths - 1)
    def _():
        start("f1")
        fed1.start()

    @pl.when(d == depths - 2)
    def _():
        start("f2")
        fed2.start()

    @pl.when(d == depths - 3)
    def _():
        for shift, copy in entering.items():
            guarded(there(MSGS["m", shift]), copy.start)

    for copy in loads:
        copy.wait()
    turned = TC[...].T
    for g in range(TABS):
        width = min(NY, table.shape[0] - g * NY)
        TT[g, :, 0:width] = turned[:, g * NY : g * NY + width]
    wraps = [d + k >= depths for k in range(3)]
    tick_row = [jnp.where(wraps[k], 2 * depths - 1 - d, depths - 1 - d) for k in range(3)] + [depths + 2 - d]
    for k in range(4):
        for g in range(TABS):
            line = TT[g, pl.ds(tick_row[k], 1), :]
            TW[k, g] = jnp.broadcast_to(line, (8, NY))

    total = strips * W
    middle = s * W + W // 2

    def lookup(count, lev, row, base, tick):
        tab = [TW[tick, g] for g in range(TABS)]

        def levels(j, nb):
            return lev[row, pl.ds(base + j, 8, stride=nb), :]

        return lambda j: looked_up(count // 8, levels, tab, j)

    def step(count, src, lead, off, coefs, dst, dst_lead):

        def load(c, j, nb):
            return src[(*lead, c, pl.ds(off + j, 8, stride=nb), slice(None))]

        def out(c, j, nb, value):
            dst[(*dst_lead, c, pl.ds(j, 8, stride=nb), slice(None))] = value

        layer(count, load, coefs, middle - count // 2, total, out)

    received("v0")
    received("a")
    step(ROWS[0], A, (), 0, lookup(ROWS[0], V0, 0, 0, 0), Y0, ())
    step(ROWS[1], Y0, (), 8, lookup(ROWS[1], V0, 1, 8, 0), Y1, (0,))
    received("v1")

    @pl.when(d == depths - 1)
    def _():
        received("f1")
        fed1.wait()

    last1 = jnp.where(d == depths - 1, 1, 0)
    step(ROWS[2], Y1, (last1,), 8, lookup(ROWS[2], V1, 0, 0, 1), Y2, ())
    copies["i1", 0, 0].start()
    step(ROWS[3], Y2, (), 8, lookup(ROWS[3], V1, 1, 8, 1), Y3, (0,))
    copies["i1", 1, 0].start()
    received("v2")

    @pl.when(d == depths - 2)
    def _():
        received("f2")
        fed2.wait()

    last2 = jnp.where(d == depths - 2, 1, 0)
    step(ROWS[4], Y3, (last2,), 8, lookup(ROWS[4], V2, 0, 0, 2), Y4, ())
    step(ROWS[5], Y4, (), 8, lookup(ROWS[5], V2, 1, 8, 2), Y5, ())

    @pl.when(d != depths - 3)
    def _():
        start("m")

    start("i2")

    def image(sources, fresh):
        def body(k, carry):
            for row in (0, 1):
                value = None if fresh else img[row, k]
                for source in sources[row]:
                    piece = product(*source, offs[k])
                    value = piece if value is None else value + piece
                img[row, k] = value
            return carry

        lax.fori_loop(0, img.shape[1], body, 0)

    def keep(ref, count, row, base):
        get = lookup(count, V0, row, base, 3)
        for j in range(count // 8):
            for c, value in enumerate(get(j)):
                ref[c, j] = value

    def kept(ref, count):
        return lambda j: [ref[c, j] for c in range(2 * ORDER + 2)]

    received("i1")
    start("e1")
    keep(C6, LAST[0], 0, 24)
    keep(C7, LAST[1], 1, 32)
    image([[(Y0, (), 48)], [(Y1, (0,), 40)]], True)
    received("e1")
    image([[(I1, (0,), 8)], [(I1, (1,), 8)]], False)
    partial_out = pltpu.make_async_copy(img, img_out, lsem.at[6])
    partial_out.start()
    lasts_out = [
        pltpu.make_async_copy(Y6.at[:, pl.ds(16, W + 16), :], last_out.at[0], lsem.at[7]),
        pltpu.make_async_copy(Y7.at[:, pl.ds(8, W + 16), :], last_out.at[1], lsem.at[8]),
    ]
    received("m")
    step(LAST[0], M, (), 0, kept(C6, LAST[0]), Y6, ())
    lasts_out[0].start()
    received("i2", 0)
    start("e2")
    step(LAST[1], Y6, (), 8, kept(C7, LAST[1]), Y7, ())
    lasts_out[1].start()
    received("i2", 1)
    received("e2")

    second_out = pltpu.make_async_copy(I2, second, lsem.at[2])
    second_out.start()

    partial_out.wait()
    second_out.wait()
    for copy in lasts_out:
        copy.wait()

    for name in copies:
        if name[0] in ("a", "v0", "v1", "v2", "i1", "i2", "e1", "e2", "m"):
            sent(name)

    @pl.when(d == depths - 1)
    def _():
        for shift in (1, -1):
            sent(("f1", shift))

    @pl.when(d == depths - 2)
    def _():
        for shift in (1, -1):
            sent(("f2", shift))


def solution(mesh):
    depths, strips = mesh.shape["depth"], mesh.shape["strip"]

    def per_device(arrivals, feed, velocity_index, offsets, coef_table):
        hbm = pl.BlockSpec(memory_space=pltpu.HBM)
        smem = pl.BlockSpec(memory_space=pltpu.SMEM)
        field = lambda n, *lead: pltpu.VMEM((*lead, 4, n, NY), F32)
        level = lambda n: pltpu.VMEM((2, n, NY), jnp.int32)
        noff = offsets.shape[0]
        columns = jnp.transpose(coef_table, (1, 2, 3, 4, 0)).reshape(-1, coef_table.shape[0])
        partial, last, second = pl.pallas_call(
            functools.partial(kernel, depths, strips),
            out_shape=(
                jax.ShapeDtypeStruct((2, noff, W, NY), F32),
                jax.ShapeDtypeStruct((2, 4, W + 16, NY), F32),
                jax.ShapeDtypeStruct((2, 4, W + 16, NY), F32),
            ),
            in_specs=[hbm, hbm, smem, hbm, hbm],
            out_specs=(hbm, hbm, hbm),
            scratch_shapes=[
                pltpu.VMEM((2, noff, W, NY), F32),
                field(128), level(128), level(96), level(64),
                field(128), field(112, 2), field(96), field(80, 2), field(64), field(48), field(80), field(64),
                field(80), field(48, 2), field(48, 2),
                pltpu.VMEM(columns.shape, F32),
                pltpu.VMEM((TABS, coef_table.shape[0], NY), F32),
                pltpu.VMEM((4, TABS, 8, NY), F32),
                pltpu.VMEM((2 * ORDER + 2, LAST[0] // 8, 8, NY), F32),
                pltpu.VMEM((2 * ORDER + 2, LAST[1] // 8, 8, NY), F32),
                pltpu.SemaphoreType.DMA((len(MSGS),)),
                pltpu.SemaphoreType.DMA((len(MSGS),)),
                pltpu.SemaphoreType.DMA((9,)),
                pltpu.SemaphoreType.REGULAR,
            ],
            compiler_params=pltpu.CompilerParams(collective_id=0, has_side_effects=True, vmem_limit_bytes=60 * 2**20),
            name="relay",
        )(arrivals, velocity_index, offsets, feed, columns)
        return pl.pallas_call(
            finish,
            out_shape=(
                jax.ShapeDtypeStruct((2, noff, W, NY), F32),
                jax.ShapeDtypeStruct((1, 1, 4, W, NY), F32),
            ),
            in_specs=[hbm, hbm, hbm, smem],
            out_specs=(hbm, hbm),
            scratch_shapes=[
                pltpu.VMEM((2, noff, W, NY), F32),
                pltpu.VMEM((2, 2, 4, W + 16, NY), F32),
                pltpu.SemaphoreType.DMA((4 * PARTS + 5,)),
            ],
            compiler_params=pltpu.CompilerParams(vmem_limit_bytes=60 * 2**20),
            name="finish",
        )(partial, last, second, offsets)

    return jax.shard_map(
        per_device,
        mesh=mesh,
        in_specs=(
            P("depth", None, None, "strip", None),
            P(None, None, None, "strip", None),
            P("depth", "strip", None),
            P(),
            P(),
        ),
        out_specs=(P("depth", None, "strip", None), P("depth", None, None, "strip", None)),
        check_vma=False,
    )
```

```python
import functools

import jax
import jax.numpy as jnp
from jax import lax
from jax.experimental import pallas as pl
from jax.experimental.pallas import tpu as pltpu
from jax.sharding import PartitionSpec as P

MESH = pl.DeviceIdType.MESH
ORDER = 8
W = 32
PARTS = 4
NY = 128
LEVELS = 32
TABS = (2 * (ORDER + 1) * LEVELS + NY - 1) // NY
F32 = jnp.float32

ROWS = (128, 112, 96, 80, 64, 48)
LAST = (80, 64)

MSGS = {}
for _s in (1, -1, 2, -2):
    MSGS["a", _s] = (0, _s)
    MSGS["v0", _s] = (0, _s)
for _s in (0, 1, -1):
    MSGS["v1", _s] = (-1, _s)
    MSGS["v2", _s] = (-2, _s)
    MSGS["m", _s] = (3, _s)
for _s in (1, -1):
    MSGS["f1", _s] = (0, _s)
    MSGS["f2", _s] = (0, _s)
    MSGS["i2", 1, _s] = (2, _s)
    MSGS["e1", _s] = (0, _s)
    MSGS["e2", _s] = (0, _s)
for _l in (0, 1):
    MSGS["i1", _l, 0] = (1, 0)
    MSGS["i2", _l, 0] = (2, 0)
INDEX = {name: i for i, name in enumerate(MSGS)}
PEERS = sorted(set(MSGS.values()))


def looked_up(nb, lev, tab, j):
    idx = lev(j, nb)
    idx = [idx + LEVELS * m for m in range(4)]
    return [jnp.take_along_axis(tab[c // 4], idx[c % 4], axis=1) for c in range(2 * ORDER + 2)]


def layer(rows, load, coefs, top, total, out):
    nb = rows // 8
    lanes = lax.broadcasted_iota(jnp.int32, (8, NY), 1)
    first, final = lanes == 0, lanes == NY - 1
    blocks = lax.broadcasted_iota(jnp.int32, (8, NY), 0) * nb + top
    inside = [(blocks + j >= 0) & (blocks + j < total) for j in range(nb)]
    quarter = [jnp.where(inside[j], 0.25, 0.0) for j in range(nb)]
    comps = range(4)
    t = [[jnp.where(inside[j], load(c, j, nb), 0.0) for j in range(nb)] for c in comps]
    hist = [t]
    p = None
    for n in range(1, ORDER + 1):
        new_t, new_p = [], []
        for c in comps:
            u = t[c]
            up = pltpu.roll(u[nb - 1], 1, 0)
            down = pltpu.roll(u[0], 7, 0)
            s = [u[j] + u[j + 1] for j in range(nb - 1)]
            tl, ql = [], []
            for j in range(nb):
                a = s[j - 1] if j else up + u[0]
                b = s[j] if j + 1 < nb else u[nb - 1] + down
                v = a + b
                sides = jnp.where(first, 0.0, pltpu.roll(v, 1, 1)) + jnp.where(
                    final, 0.0, pltpu.roll(v, NY - 1, 1)
                )
                q = (v + v) + sides
                if n == 1:
                    r = q * (quarter[j] * 0.5)
                else:
                    r = q * quarter[j] - p[c][j]
                ql.append(r)
                tl.append(r - u[j])
            new_t.append(tl)
            new_p.append(ql)
        t, p = new_t, new_p
        hist.append(t)
    for j in range(nb):
        chosen = coefs(j)
        acc = [None] * 4
        for n in range(ORDER + 1):
            cr, ci = chosen[2 * n], chosen[2 * n + 1]
            sr, si, rr, ri = [hist[n][c][j] for c in comps]
            new = [
                cr * sr - ci * si,
                cr * si + ci * sr,
                cr * rr + ci * ri,
                cr * ri - ci * rr,
            ]
            acc = [new[c] if n == 0 else acc[c] + new[c] for c in comps]
        for c in comps:
            out(c, j, nb, acc[c])


def product(ref, lead, at, h):
    low = [ref[(*lead, c, pl.ds(at - h, W), slice(None))] for c in (0, 1)]
    high = [ref[(*lead, c, pl.ds(at + h, W), slice(None))] for c in (2, 3)]
    return low[0] * high[0] + low[1] * high[1]


def finish(partial, last, second, offs, image, outflow, out, sem):
    stores = [pltpu.make_async_copy(last.at[1, :, pl.ds(8, W), :], outflow.at[0, 0], sem.at[0])]
    stores[0].start()
    count = out.shape[1] // PARTS
    for row in (0, 1):
        for part in range(PARTS):
            for k in range(part * count, part * count + count):
                h = offs[k]
                out[row, k] = partial[row, k] + product(last, (row,), 8, h) + product(second, (row,), 8, h)
            some = pl.ds(part * count, count)
            stores.append(pltpu.make_async_copy(out.at[row, some], image.at[row, some], sem.at[len(stores)]))
            stores[-1].start()
    for copy in stores:
        copy.wait()


def kernel(depths, strips, arr, vel, offs, feed, table, img, last, second, A, V0, V1, V2, Y0, Y1, Y2, Y3, Y4, Y5, Y6, Y7, M, I1, I2, TC, TT, TW, C6, C7, ssem, rsem, lsem):
    d = lax.axis_index("depth")
    s = lax.axis_index("strip")

    def peer(shift):
        return (
            lax.rem(d + shift[0] + depths, depths),
            s + shift[1],
        )

    def there(shift, sign=1):
        if shift[1] == 0:
            return None
        at = s + sign * shift[1]
        return (at >= 0) & (at < strips)

    def guarded(condition, action):
        if condition is None:
            action()
        else:
            pl.when(condition)(action)

    loads = [
        pltpu.make_async_copy(table, TC, lsem.at[3]),
        pltpu.make_async_copy(arr.at[0, 0], A.at[:, pl.ds(48, 32), :], lsem.at[4]),
        pltpu.make_async_copy(vel, V0.at[:, pl.ds(48, 32), :], lsem.at[5]),
    ]
    for copy in loads:
        copy.start()

    @pl.when(s < 2)
    def _():
        V0[:, 0:48, :] = jnp.zeros((2, 48, NY), jnp.int32)
        V1[:, 0:32, :] = jnp.zeros((2, 32, NY), jnp.int32)
        V2[:, 0:16, :] = jnp.zeros((2, 16, NY), jnp.int32)

    @pl.when(s >= strips - 2)
    def _():
        V0[:, 80:128, :] = jnp.zeros((2, 48, NY), jnp.int32)
        V1[:, 64:96, :] = jnp.zeros((2, 32, NY), jnp.int32)
        V2[:, 48:64, :] = jnp.zeros((2, 16, NY), jnp.int32)

    for end, at in ((0, 0), (strips - 1, 40)):
        @pl.when(s == end)
        def _(at=at):
            for ref in (I1, I2):
                ref[:, :, at : at + 8, :] = jnp.zeros((2, 4, 8, NY), F32)

    barrier = pltpu.get_barrier_semaphore()
    expected = 0
    for shift in PEERS:
        def greet(shift=shift):
            pl.semaphore_signal(barrier, inc=1, device_id=peer((-shift[0], -shift[1])), device_id_type=MESH)

        guarded(there(shift, -1), greet)
        expected = expected + (1 if shift[1] == 0 else jnp.where(there(shift), 1, 0))

    def send(name, src, dst):
        i = INDEX[name]
        return pltpu.make_async_remote_copy(
            src_ref=src, dst_ref=dst, send_sem=ssem.at[i], recv_sem=rsem.at[i],
            device_id=peer(MSGS[name]), device_id_type=MESH,
        )

    def rows(ref, start, count, lead=()):
        return ref.at[(*lead, slice(None), pl.ds(start, count), slice(None))]

    own = arr.at[0, 0]
    lead1, lead2 = A.shape[1] // 2 - W // 2, V2.shape[1] // 2 - W // 2
    sends = {}
    sends["v0", 1] = (vel, rows(V0, 16, 32))
    sends["v0", -1] = (vel, rows(V0, 80, 32))
    sends["v0", 2] = (rows(vel, 16, 16), rows(V0, 0, 16))
    sends["v0", -2] = (rows(vel, 0, 16), rows(V0, 112, 16))
    sends["a", 1] = (own, rows(A, 16, 32))
    sends["a", -1] = (own, rows(A, 80, 32))
    sends["a", 2] = (rows(arr, 16, 16, (0, 0)), rows(A, 0, 16))
    sends["a", -2] = (rows(arr, 0, 16, (0, 0)), rows(A, 112, 16))
    sends["v1", 0] = (vel, rows(V1, 32, 32))
    sends["v1", 1] = (vel, rows(V1, 0, 32))
    sends["v1", -1] = (vel, rows(V1, 64, 32))
    sends["v2", 0] = (vel, rows(V2, 16, 32))
    sends["v2", 1] = (rows(vel, 16, 16), rows(V2, 0, 16))
    sends["v2", -1] = (rows(vel, 0, 16), rows(V2, 48, 16))
    for layer_ in (0, 1):
        sends["i1", layer_, 0] = (
            rows((Y2, Y3)[layer_], (32, 24)[layer_], 32, () if layer_ == 0 else (0,)),
            rows(I1, 8, 32, (layer_,)),
        )
    sends["i2", 0, 0] = (rows(Y4, 16, 32), rows(I2, 8, 32, (0,)))
    for shift, at, to in ((1, 32, 0), (-1, 8, 40)):
        sends["e1", shift] = [I1.at[:, :, pl.ds(row, 8), :] for row in (at, to)]
        sends["e2", shift] = [rows(I2, row, 8, (0,)) for row in (at, to)]
    sends["i2", 1, 0] = (rows(Y5, 8, 32), rows(I2, 8, 32, (1,)))
    sends["i2", 1, 1] = (rows(Y5, 32, 8), rows(I2, 0, 8, (1,)))
    sends["i2", 1, -1] = (rows(Y5, 8, 8), rows(I2, 40, 8, (1,)))
    moved = {0: (8, 32, 24), 1: (16, 24, 0), -1: (8, 24, 56)}
    for shift, (start, count, to) in moved.items():
        sends["m", shift] = (rows(Y5, start, count), rows(M, to, count))
    for shift, to in ((1, 8), (-1, 72)):
        sends["f1", shift] = (feed.at[0, 0], rows(Y1, to, 32, (1,)))
    sends["f2", 1] = (rows(feed, 16, 16, (1, 0)), rows(Y3, 8, 16, (1,)))
    sends["f2", -1] = (rows(feed, 0, 16, (1, 0)), rows(Y3, 56, 16, (1,)))
    copies = {name: send(name, *ends) for name, ends in sends.items()}

    def start(kind):
        for name in copies:
            if name[0] == kind:
                guarded(there(MSGS[name]), copies[name].start)

    def received(*kind):
        for name in copies:
            if name[: len(kind)] == kind:
                guarded(there(MSGS[name], -1), copies[name].wait_recv)

    def sent(name):
        guarded(there(MSGS[name]), copies[name].wait_send)

    fed1 = pltpu.make_async_copy(feed.at[0, 0], rows(Y1, 40, 32, (1,)), lsem.at[0])
    fed2 = pltpu.make_async_copy(feed.at[1, 0], rows(Y3, 24, 32, (1,)), lsem.at[1])
    entering = {}
    for shift, (at, count, to) in moved.items():
        entering[shift] = send(("m", shift), rows(feed, at - 8, count, (2, 0)), rows(M, to, count))

    pl.semaphore_wait(barrier, expected)
    start("v0")
    start("a")
    start("v1")
    start("v2")

    @pl.when(d == depths - 1)
    def _():
        start("f1")
        fed1.start()

    @pl.when(d == depths - 2)
    def _():
        start("f2")
        fed2.start()

    @pl.when(d == depths - 3)
    def _():
        for shift, copy in entering.items():
            guarded(there(MSGS["m", shift]), copy.start)

    for copy in loads:
        copy.wait()
    turned = TC[...].T
    for g in range(TABS):
        width = min(NY, table.shape[0] - g * NY)
        TT[g, :, 0:width] = turned[:, g * NY : g * NY + width]
    wraps = [d + k >= depths for k in range(3)]
    tick_row = [jnp.where(wraps[k], 2 * depths - 1 - d, depths - 1 - d) for k in range(3)] + [depths + 2 - d]
    for k in range(4):
        for g in range(TABS):
            line = TT[g, pl.ds(tick_row[k], 1), :]
            TW[k, g] = jnp.broadcast_to(line, (8, NY))

    total = strips * W
    middle = s * W + W // 2

    def lookup(count, lev, row, base, tick):
        tab = [TW[tick, g] for g in range(TABS)]

        def levels(j, nb):
            return lev[row, pl.ds(base + j, 8, stride=nb), :]

        return lambda j: looked_up(count // 8, levels, tab, j)

    def step(count, src, lead, off, coefs, dst, dst_lead):

        def load(c, j, nb):
            return src[(*lead, c, pl.ds(off + j, 8, stride=nb), slice(None))]

        def out(c, j, nb, value):
            dst[(*dst_lead, c, pl.ds(j, 8, stride=nb), slice(None))] = value

        layer(count, load, coefs, middle - count // 2, total, out)

    received("v0")
    received("a")
    step(ROWS[0], A, (), 0, lookup(ROWS[0], V0, 0, 0, 0), Y0, ())
    step(ROWS[1], Y0, (), 8, lookup(ROWS[1], V0, 1, 8, 0), Y1, (0,))
    received("v1")

    @pl.when(d == depths - 1)
    def _():
        received("f1")
        fed1.wait()

    last1 = jnp.where(d == depths - 1, 1, 0)
    step(ROWS[2], Y1, (last1,), 8, lookup(ROWS[2], V1, 0, 0, 1), Y2, ())
    copies["i1", 0, 0].start()
    step(ROWS[3], Y2, (), 8, lookup(ROWS[3], V1, 1, 8, 1), Y3, (0,))
    copies["i1", 1, 0].start()
    received("v2")

    @pl.when(d == depths - 2)
    def _():
        received("f2")
        fed2.wait()

    last2 = jnp.where(d == depths - 2, 1, 0)
    step(ROWS[4], Y3, (last2,), 8, lookup(ROWS[4], V2, 0, 0, 2), Y4, ())
    step(ROWS[5], Y4, (), 8, lookup(ROWS[5], V2, 1, 8, 2), Y5, ())

    @pl.when(d != depths - 3)
    def _():
        start("m")

    start("i2")

    def image(sources, fresh):
        def body(k, carry):
            for row in (0, 1):
                value = None if fresh else img[row, k]
                for source in sources[row]:
                    piece = product(*source, offs[k])
                    value = piece if value is None else value + piece
                img[row, k] = value
            return carry

        lax.fori_loop(0, img.shape[1], body, 0)

    def keep(ref, count, row, base):
        get = lookup(count, V0, row, base, 3)
        for j in range(count // 8):
            for c, value in enumerate(get(j)):
                ref[c, j] = value

    def kept(ref, count):
        return lambda j: [ref[c, j] for c in range(2 * ORDER + 2)]

    received("i1")
    start("e1")
    keep(C6, LAST[0], 0, 24)
    keep(C7, LAST[1], 1, 32)
    image([[(Y0, (), 48)], [(Y1, (0,), 40)]], True)
    received("e1")
    image([[(I1, (0,), 8)], [(I1, (1,), 8)]], False)
    received("m")
    step(LAST[0], M, (), 0, kept(C6, LAST[0]), Y6, ())
    received("i2", 0)
    start("e2")
    step(LAST[1], Y6, (), 8, kept(C7, LAST[1]), Y7, ())
    last[0] = Y6[:, 16:64, :]
    last[1] = Y7[:, 8:56, :]
    received("i2", 1)
    received("e2")

    second[...] = I2[...]

    for name in copies:
        if name[0] in ("a", "v0", "v1", "v2", "i1", "i2", "e1", "e2", "m"):
            sent(name)

    @pl.when(d == depths - 1)
    def _():
        for shift in (1, -1):
            sent(("f1", shift))

    @pl.when(d == depths - 2)
    def _():
        for shift in (1, -1):
            sent(("f2", shift))


def solution(mesh):
    depths, strips = mesh.shape["depth"], mesh.shape["strip"]

    def per_device(arrivals, feed, velocity_index, offsets, coef_table):
        hbm = pl.BlockSpec(memory_space=pltpu.HBM)
        vmem = pl.BlockSpec(memory_space=pltpu.VMEM)
        smem = pl.BlockSpec(memory_space=pltpu.SMEM)
        field = lambda n, *lead: pltpu.VMEM((*lead, 4, n, NY), F32)
        level = lambda n: pltpu.VMEM((2, n, NY), jnp.int32)
        noff = offsets.shape[0]
        columns = jnp.transpose(coef_table, (1, 2, 3, 4, 0)).reshape(-1, coef_table.shape[0])
        partial, last, second = pl.pallas_call(
            functools.partial(kernel, depths, strips),
            out_shape=(
                jax.ShapeDtypeStruct((2, noff, W, NY), F32),
                jax.ShapeDtypeStruct((2, 4, W + 16, NY), F32),
                jax.ShapeDtypeStruct((2, 4, W + 16, NY), F32),
            ),
            in_specs=[hbm, hbm, smem, hbm, hbm],
            out_specs=(vmem, vmem, vmem),
            scratch_shapes=[
                field(128), level(128), level(96), level(64),
                field(128), field(112, 2), field(96), field(80, 2), field(64), field(48), field(80), field(64),
                field(80), field(48, 2), field(48, 2),
                pltpu.VMEM(columns.shape, F32),
                pltpu.VMEM((TABS, coef_table.shape[0], NY), F32),
                pltpu.VMEM((4, TABS, 8, NY), F32),
                pltpu.VMEM((2 * ORDER + 2, LAST[0] // 8, 8, NY), F32),
                pltpu.VMEM((2 * ORDER + 2, LAST[1] // 8, 8, NY), F32),
                pltpu.SemaphoreType.DMA((len(MSGS),)),
                pltpu.SemaphoreType.DMA((len(MSGS),)),
                pltpu.SemaphoreType.DMA((9,)),
            ],
            compiler_params=pltpu.CompilerParams(collective_id=0, has_side_effects=True, vmem_limit_bytes=40 * 2**20),
            name="relay",
        )(arrivals, velocity_index, offsets, feed, columns)
        return pl.pallas_call(
            finish,
            out_shape=(
                jax.ShapeDtypeStruct((2, noff, W, NY), F32),
                jax.ShapeDtypeStruct((1, 1, 4, W, NY), F32),
            ),
            in_specs=[vmem, vmem, vmem, smem],
            out_specs=(hbm, hbm),
            scratch_shapes=[
                pltpu.VMEM((2, noff, W, NY), F32),
                pltpu.SemaphoreType.DMA((2 * PARTS + 1,)),
            ],
            compiler_params=pltpu.CompilerParams(vmem_limit_bytes=8 * 2**20),
            name="finish",
        )(partial, last, second, offsets)

    return jax.shard_map(
        per_device,
        mesh=mesh,
        in_specs=(
            P("depth", None, None, "strip", None),
            P(None, None, None, "strip", None),
            P("depth", "strip", None),
            P(),
            P(),
        ),
        out_specs=(P("depth", None, "strip", None), P("depth", None, None, "strip", None)),
        check_vma=False,
    )
```
